32 devices in a mesh: px: 8 (over y, x, core), py: 4 (over z).
Axes of the slice: x: 2, y: 2, z: 4, core: 2. Of those that a mesh axis runs over, the one named last changes fastest.
Arguments:
- moving_image: float32 [8, 128, 2048], P(None, 'px', 'py'), may hold values from -6 to 6
- fixed_image: bfloat16 [8, 128, 2048], P(None, 'px', 'py'), may hold values from -6 to 6
- departures: int32 [8, 128, 2048], P(None, 'px', 'py'), may hold values from 0 to 63
Outputs:
- velocity_grad: bfloat16 [3, 8, 128, 2048], P(None, None, 'px', 'py')
The draws below stay inside these ranges and needn't reach their ends.
Inputs may be any that keep to these rules, and one draw needn't show every extreme that they name: `departures`: each value encodes offsets (oz, ox, oy), each from -2 to 1, as ((oz + 2) * 2 * 2 + ox + 2) * 2 * 2 + oy + 2.
All inputs are finite; a program needn't handle non-finite values.
Results may differ from the reference program's by a relative error of at most 0.001.
Values sent between devices are 32-bit elements; how exact they have to be, the bound alone decides.
No kernel may reach another device: no remote copies, remote signals or barrier semaphores. Data moves between devices by JAX's collectives and lax.ppermute only.
A program may use at most 64 MiB of HBM per device.

```python
import jax
import jax.numpy as jnp
from jax import lax

REACH = 2
PLANES = 8
NX = 128
NY = 2048


def plant(drawn, key, least, high):
    longest = drawn.shape.index(max(drawn.shape))
    spots = []
    for shift in (0, 1):
        where = [jax.random.randint(jax.random.fold_in(key, axis), (), 0, length) for axis, length in enumerate(drawn.shape)]
        where[longest] = (where[longest] + shift) % drawn.shape[longest]
        spots.append(tuple(where))
    return drawn.at[spots[0]].set(least).at[spots[1]].set(high)


def shard_levels(key, shape, pieces, low, largest):
    factor_of = 1.0
    for axis_at, parts in pieces:
        heights = jax.random.uniform(jax.random.fold_in(jax.random.fold_in(key, 6), axis_at), (parts,), jnp.float32, low / len(pieces), largest / len(pieces))
        factor_of = factor_of * jnp.repeat(jnp.exp(heights), shape[axis_at] // parts).reshape((-1,) + (1,) * (len(shape) - 1 - axis_at))
    return factor_of


def centred(rng, shape, width, bound, shards=(), kind=jnp.bfloat16):
    gain = shard_levels(rng, shape, shards, -0.22, 0.18) if shards else 1.0
    values = jax.random.normal(rng, shape, jnp.float32) * width * gain
    return jnp.minimum(jnp.maximum(values, -bound), bound).astype(kind)


def setup_inputs(seed: int = 0) -> dict:
    streams_of = jax.random.split(jax.random.key(seed), 4)
    return {
        "moving_image": centred(streams_of[0], (PLANES, NX, NY), 1.0, 6.0, ((1, 8), (2, 4)), jnp.float32),
        "fixed_image": centred(streams_of[1], (PLANES, NX, NY), 1.0, 6.0, ((1, 8), (2, 4))),
        "departures": plant(jax.random.randint(streams_of[2], (PLANES, NX, NY), 0, 8 * REACH ** 3), jax.random.fold_in(streams_of[2], 1), 0, (8 * REACH ** 3) - 1).astype(jnp.int32),
    }


frac_z = 0.25
frac_x = 0.375
frac_y = 0.625
filter_taps = (0.0625, 0.25, 0.375, 0.25, 0.0625)


def corner_list():
    corners = []
    for shift_z in (0, 1):
        for shift_x in (0, 1):
            for shift_y in (0, 1):
                weight = (frac_z if shift_z else 1.0 - frac_z) * (frac_x if shift_x else 1.0 - frac_x) * (frac_y if shift_y else 1.0 - frac_y)
                corners.append((shift_z, shift_x, shift_y, weight))
    return corners


def flat_indices(departures, double):
    planes, row_count, col_count = departures.shape
    wide_rows = row_count + double
    wide_cols = col_count + double
    off_y = departures % double
    off_x = (departures // double) % double
    off_z = departures // (double * double)
    base_z = jnp.arange(planes, dtype=jnp.int32)[:, None, None] + off_z
    base_x = jnp.arange(row_count, dtype=jnp.int32)[None, :, None] + off_x
    base_y = jnp.arange(col_count, dtype=jnp.int32)[None, None, :] + off_y
    result = []
    for shift_z, shift_x, shift_y, weight in corner_list():
        flat_index = ((base_z + shift_z) * wide_rows + base_x + shift_x) * wide_cols + base_y + shift_y
        result.append((flat_index.astype(jnp.int32), weight))
    return result


def sample(padded, departures, double):
    flat = padded.reshape(-1)
    summed = jnp.zeros(departures.shape, jnp.float32)
    for flat_index, weight in flat_indices(departures, double):
        summed = summed + weight * jnp.take(flat, flat_index)
    return summed


def spread(values, departures, double):
    planes, row_count, col_count = departures.shape
    buffer = jnp.zeros(((planes + double) * (row_count + double) * (col_count + double),), jnp.float32)
    for flat_index, weight in flat_indices(departures, double):
        buffer = buffer.at[flat_index.reshape(-1)].add((weight * values).reshape(-1))
    return buffer.reshape(planes + double, row_count + double, col_count + double)


def advect(volume, departures):
    double = 2 * REACH
    padded = jnp.pad(volume, REACH)

    def plane(plane_index):
        slab_planes = lax.dynamic_slice_in_dim(padded, plane_index, double + 1, 0)
        code_plane = lax.dynamic_slice_in_dim(departures, plane_index, 1, 0)
        return sample(slab_planes, code_plane, double)[0]

    return lax.map(plane, jnp.arange(PLANES, dtype=jnp.int32))


def advect_adjoint(values, departures):
    double = 2 * REACH
    accum_pad = jnp.zeros((PLANES + double, NX + double, NY + double), jnp.float32)

    def turn(accum_now, plane_index):
        part = spread(lax.dynamic_slice_in_dim(values, plane_index, 1, 0), lax.dynamic_slice_in_dim(departures, plane_index, 1, 0), double)
        before = lax.dynamic_slice_in_dim(accum_now, plane_index, double + 1, 0)
        return lax.dynamic_update_slice_in_dim(accum_now, before + part, plane_index, 0), None

    accum_pad, unused = lax.scan(turn, accum_pad, jnp.arange(PLANES, dtype=jnp.int32))
    return accum_pad[REACH:REACH + PLANES, REACH:REACH + NX, REACH:REACH + NY]


def derivative(volume, along):
    extent = volume.shape[along]
    padded = jnp.pad(volume, [(1, 1) if dim_index == along else (0, 0) for dim_index in range(volume.ndim)])
    return (lax.slice_in_dim(padded, 2, 2 + extent, axis=along) - lax.slice_in_dim(padded, 0, extent, axis=along)) * 0.5


def taps_valid(widened, along, extent):
    summed = filter_taps[0] * lax.slice_in_dim(widened, 0, extent, axis=along)
    for offset in range(1, 5):
        summed = summed + filter_taps[offset] * lax.slice_in_dim(widened, offset, offset + extent, axis=along)
    return summed


def smooth_axis(values, along):
    padded = jnp.pad(values, [(2, 2) if dim_index == along else (0, 0) for dim_index in range(values.ndim)])
    return taps_valid(padded, along, values.shape[along])


def reference(moving_image, fixed_image, departures):
    image_one = advect(moving_image, departures)
    image_two = advect(image_one, departures)
    adjoint_last = image_two - fixed_image.astype(jnp.float32)
    adjoint_one = advect_adjoint(adjoint_last, departures)
    components_out = []
    for component in range(3):
        raw_grad = -(adjoint_last * derivative(image_one, component) + adjoint_one * derivative(moving_image, component))
        smoothed = smooth_axis(smooth_axis(smooth_axis(raw_grad, 0), 1), 2)
        components_out.append(smoothed.astype(jnp.bfloat16))
    return jnp.stack(components_out)
```

```python
import functools

import jax
import jax.numpy as jnp
from jax import lax
from jax.experimental import pallas as pl
from jax.experimental.pallas import tpu as pltpu
from jax.sharding import PartitionSpec as P

LANES = 128
HALO = 8
FIXED_HALO = 4
CODE_HALO = 6
SLAB = HALO + CODE_HALO + FIXED_HALO
VMEM = 60 * 1024 * 1024

Z1, X1, Y1 = 0.25, 0.375, 0.625
Z0, X0, Y0 = 1.0 - Z1, 1.0 - X1, 1.0 - Y1


def roll(value, shift):
    return pltpu.roll(value, shift % LANES, 1)


def shifted(blocks, step, lane):
    if step == 0:
        return blocks
    rolled = [roll(block, -step) for block in blocks]
    count = len(blocks)
    if step > 0:
        return [jnp.where(lane < LANES - step, rolled[b], rolled[(b + 1) % count]) for b in range(count)]
    return [jnp.where(lane >= -step, rolled[b], rolled[(b - 1) % count]) for b in range(count)]


def pack_columns(moving, fixed, codes, edge):
    planes, rows, cols = moving.shape
    lane = lax.broadcasted_iota(jnp.int32, (rows, LANES), 1)

    def ring(first, last):
        return jnp.where(lane < LANES // 2, first, last)

    def plane(z, _):
        image = ring(moving[z, :, :LANES], moving[z, :, cols - LANES :])
        code = ring(codes[z, :, :LANES], codes[z, :, cols - LANES :]).astype(jnp.float32)
        target = ring(fixed[z, :, :LANES].astype(jnp.float32), fixed[z, :, cols - LANES :].astype(jnp.float32))
        code = roll(code, 2 * HALO)
        target = roll(target, 4 * HALO)
        packed = jnp.where((lane >= HALO) & (lane < 3 * HALO), code, image)
        packed = jnp.where((lane >= 3 * HALO) & (lane < 5 * HALO), target, packed)
        edge[z] = packed
        return 0

    lax.fori_loop(0, planes, plane, 0, unroll=True)


def merged_edge(from_left, from_right, z, lane):
    left = (lane >= LANES - HALO) | ((lane >= HALO) & (lane < 2 * HALO)) | ((lane >= 3 * HALO) & (lane < 4 * HALO))
    return jnp.where(left, from_left[z], from_right[z])


def pack_rows(moving, fixed, codes, from_left, from_right, first, last):
    planes, rows, cols = moving.shape
    blocks = cols // LANES
    lane = lax.broadcasted_iota(jnp.int32, (rows, LANES), 1)

    def plane(z, _):
        for b in range(blocks):
            at = slice(b * LANES, (b + 1) * LANES)
            image = moving[z, :, at]
            code = codes[z, :, at].astype(jnp.float32)
            target = fixed[z, :, at].astype(jnp.float32)
            row = b * SLAB
            first[z, row : row + HALO] = image[:HALO]
            first[z, row + HALO : row + HALO + CODE_HALO] = code[:CODE_HALO]
            first[z, row + HALO + CODE_HALO : row + SLAB] = target[:FIXED_HALO]
            last[z, row : row + HALO] = image[rows - HALO :]
            last[z, row + HALO : row + HALO + CODE_HALO] = code[rows - CODE_HALO :]
            last[z, row + HALO + CODE_HALO : row + SLAB] = target[rows - FIXED_HALO :]
        edge = merged_edge(from_left, from_right, z, lane)
        first[z, blocks * SLAB :] = edge[:HALO]
        last[z, blocks * SLAB :] = edge[rows - HALO :]
        return 0

    lax.fori_loop(0, planes, plane, 0)


def gradient(
    peers, moving, fixed, codes, from_left, from_right, lower, upper, out, image, first, code, target, table, parts, last, carried, raw
):
    planes, rows, cols = moving.shape
    inner = cols // LANES
    blocks = inner + 1
    f32 = jnp.float32
    lane = lax.broadcasted_iota(jnp.int32, (8, LANES), 1)
    row_at = lax.broadcasted_iota(jnp.int32, (8, LANES), 0)
    at_x, at_y = lax.axis_index("px"), lax.axis_index("py")
    least = jnp.where(at_x > 0, -HALO, 0)
    most = jnp.where(at_x < peers[0] - 1, rows + HALO, rows)
    has_left = (at_y > 0).astype(f32)
    has_right = (at_y < peers[1] - 1).astype(f32)
    ring_valid = jnp.where(lane < LANES // 2, has_right, has_left)

    def valid(x, b):
        row_valid = None
        if x < 0 or x + 8 > rows:
            row_valid = jnp.where((row_at + x >= least) & (row_at + x < most), 1.0, 0.0)
        if b < inner:
            return row_valid
        return ring_valid if row_valid is None else row_valid * ring_valid

    def inside(value, x, b):
        factor = valid(x, b)
        return value if factor is None else value * factor

    def group(x):
        return slice(x + HALO, x + HALO + 8)

    zeros = jnp.zeros((blocks, 32, LANES), f32)
    for ref, spots in ((image, (0, planes + 1)), (first, (0, planes + 1))):
        for spot in spots:
            ref[spot] = zeros
    for o in range(4):
        for spot in (0, planes + 2):
            table[o, spot] = zeros
        for spot in (0, 1, planes + 2, planes + 3):
            parts[o, spot] = zeros
            if o < 3:
                raw[o, spot] = zeros

    own = slice(HALO, HALO + rows)
    wide_lane = lax.broadcasted_iota(jnp.int32, (rows, LANES), 1)

    def gather_plane(z, _):
        for b in range(inner):
            at = slice(b * LANES, (b + 1) * LANES)
            image[z + 1, b, own] = moving[z, :, at]
            code[z + 2, b, own] = codes[z, :, at]
            target[z, b, own] = fixed[z, :, at].astype(f32)
            row = b * SLAB
            for slab, start in ((lower, True), (upper, False)):
                a = row + HALO
                c = a + CODE_HALO
                d = c + FIXED_HALO
                if start:
                    image[z + 1, b, 0:HALO] = slab[z, row:a]
                    code[z + 2, b, HALO - CODE_HALO : HALO] = slab[z, a:c].astype(jnp.int32)
                    target[z, b, HALO - FIXED_HALO : HALO] = slab[z, c:d]
                else:
                    end = HALO + rows
                    image[z + 1, b, end : end + HALO] = slab[z, row:a]
                    code[z + 2, b, end : end + CODE_HALO] = slab[z, a:c].astype(jnp.int32)
                    target[z, b, end : end + FIXED_HALO] = slab[z, c:d]
        edges = (
            (own, merged_edge(from_left, from_right, z, wide_lane)),
            (slice(0, HALO), lower[z, inner * SLAB :]),
            (slice(HALO + rows, HALO + rows + HALO), upper[z, inner * SLAB :]),
        )
        for at, edge in edges:
            image[z + 1, inner, at] = edge
            code[z + 2, inner, at] = roll(edge, -2 * HALO).astype(jnp.int32)
            target[z, inner, at] = roll(edge, -4 * HALO)
        return 0

    lax.fori_loop(0, planes, gather_plane, 0)

    def fill_table(source, starts):
        def plane(z, _):
            for x in starts:
                at, up = group(x), group(x + 1)
                sums = [
                    (Z0 * X0) * source[z, b, at]
                    + (Z0 * X1) * source[z, b, up]
                    + (Z1 * X0) * source[z + 1, b, at]
                    + (Z1 * X1) * source[z + 1, b, up]
                    for b in range(blocks)
                ]
                moved = {step: shifted(sums, step, lane) for step in range(-2, 3)}
                for o in range(4):
                    for b in range(blocks):
                        table[o, z + 1, b, at] = Y0 * moved[o - 2][b] + Y1 * moved[o - 1][b]
            return 0

        lax.fori_loop(0, planes + 1, plane, 0)

    def masks(value):
        return [(value & (1 << bit)) != 0 for bit in range(6)]

    def pick(z, b, x, bits):
        def level(oz, ox):
            at = group(x + ox - 2)
            options = [table[oy, z + oz, b, at] for oy in range(4)]
            return jnp.where(bits[1], jnp.where(bits[0], options[3], options[2]), jnp.where(bits[0], options[1], options[0]))

        def row_level(oz):
            options = [level(oz, ox) for ox in range(4)]
            return jnp.where(bits[3], jnp.where(bits[2], options[3], options[2]), jnp.where(bits[2], options[1], options[0]))

        options = [row_level(oz) for oz in range(4)]
        return jnp.where(bits[5], jnp.where(bits[4], options[3], options[2]), jnp.where(bits[4], options[1], options[0]))

    fill_table(image, (-8, 0, 8, 15))

    def first_plane(z, _):
        for b in range(blocks):
            for x in (-6, 2, 6, 14):
                value = pick(z, b, x, masks(code[z + 2, b, group(x)]))
                first[z + 1, b, group(x)] = inside(value, x, b)
        return 0

    lax.fori_loop(0, planes, first_plane, 0)

    fill_table(first, (-6, 2, 10, 13))

    def second_plane(z, _):
        for b in range(blocks):
            for x in (-4, 4, 12):
                at = group(x)
                spot = code[z + 2, b, at]
                value = pick(z, b, x, masks(spot)) - target[z, b, at]
                value = inside(value, x, b)
                last[z, b, at] = value
                along = spot & 3
                for o in range(4):
                    parts[o, z + 2, b, at] = jnp.where(along == o, value, 0.0)
                code[z + 2, b, at] = lax.shift_right_logical(spot, 2)
        return 0

    lax.fori_loop(0, planes, second_plane, 0)

    def carry_plane(z, _):
        for x in (-3, 5, 10):
            landed = [[], [], [], []]
            for b in range(blocks):
                sums = [None] * 4
                for oz in range(4):
                    for ox in range(4):
                        at = group(x + 2 - ox)
                        here = code[z + 3 - oz, b, at] == oz * 4 + ox
                        for oy in range(4):
                            term = jnp.where(here, parts[oy, z + 3 - oz, b, at], 0.0)
                            sums[oy] = term if sums[oy] is None else sums[oy] + term
                for oy in range(4):
                    landed[oy].append(sums[oy])
            total = None
            for step in range(-2, 3):
                low, high = step + 2, step + 1
                terms = []
                for b in range(blocks):
                    term = Y0 * landed[low][b] if low < 4 else None
                    if high >= 0:
                        more = Y1 * landed[high][b]
                        term = more if term is None else term + more
                    terms.append(term)
                terms = shifted(terms, -step, lane)
                total = terms if total is None else [s + t for s, t in zip(total, terms)]
            for b in range(blocks):
                carried[z, b, group(x)] = total[b]
        return 0

    lax.fori_loop(0, planes + 1, carry_plane, 0)

    def raw_plane(z, _):
        for x in (-2, 6, 10):
            at, below, above = group(x), group(x - 1), group(x + 1)
            slope_one = [first[z + 1, b, at] for b in range(blocks)]
            slope_zero = [image[z + 1, b, at] for b in range(blocks)]
            slope_one = [s - t for s, t in zip(shifted(slope_one, 1, lane), shifted(slope_one, -1, lane))]
            slope_zero = [s - t for s, t in zip(shifted(slope_zero, 1, lane), shifted(slope_zero, -1, lane))]
            for b in range(blocks):
                one = inside(last[z, b, at], x, b)
                two = (
                    (Z0 * X0) * carried[z + 1, b, at]
                    + (Z0 * X1) * carried[z + 1, b, below]
                    + (Z1 * X0) * carried[z, b, at]
                    + (Z1 * X1) * carried[z, b, below]
                )
                two = inside(two, x, b)
                raw[0, z + 2, b, at] = one * (first[z + 2, b, at] - first[z, b, at]) + two * (image[z + 2, b, at] - image[z, b, at])
                raw[1, z + 2, b, at] = one * (first[z + 1, b, above] - first[z + 1, b, below]) + two * (
                    image[z + 1, b, above] - image[z + 1, b, below]
                )
                raw[2, z + 2, b, at] = one * slope_one[b] + two * slope_zero[b]
        return 0

    lax.fori_loop(0, planes, raw_plane, 0)

    def taps(a, b, c, d, e):
        return (a + e) + 4.0 * (b + d) + 6.0 * c

    def rows_plane(z, _):
        for k in range(3):
            for b in range(blocks):
                for x in range(0, rows, 8):
                    table[k, z, b, group(x)] = taps(*[raw[k, z, b, group(x + s)] for s in range(-2, 3)])
        return 0

    lax.fori_loop(0, planes + 4, rows_plane, 0)

    scale = -0.5 / 4096.0

    def out_plane(z, _):
        for k in range(3):
            halves = []
            for x in range(0, rows, 8):
                values = [taps(*[table[k, z + s, b, group(x)] for s in range(5)]) for b in range(blocks)]
                moved = [shifted(values, step, lane) for step in range(-2, 3)]
                halves.append([taps(*[m[b] for m in moved]) * scale for b in range(inner)])
            for b in range(inner):
                both = jnp.concatenate([half[b] for half in halves], axis=0)
                out[k, z, :, b * LANES : (b + 1) * LANES] = both.astype(out.dtype)
        return 0

    lax.fori_loop(0, planes, out_plane, 0)


def neighbours(value, axis):
    count = lax.axis_size(axis)
    up = [(i, i + 1) for i in range(count - 1)]
    down = [(i + 1, i) for i in range(count - 1)]
    first, last = value
    return lax.ppermute(last, axis, up), lax.ppermute(first, axis, down)


def shards(moving, fixed, codes):
    planes, rows, cols = moving.shape
    blocks = cols // LANES + 1
    f32 = jnp.float32
    params = pltpu.CompilerParams(vmem_limit_bytes=VMEM)
    edge = pl.pallas_call(
        pack_columns, out_shape=jax.ShapeDtypeStruct((planes, rows, LANES), f32), compiler_params=params
    )(moving, fixed, codes)
    from_left, from_right = neighbours((edge, edge), "py")
    slab = jax.ShapeDtypeStruct((planes, (blocks - 1) * SLAB + HALO, LANES), f32)
    slabs = pl.pallas_call(pack_rows, out_shape=(slab, slab), compiler_params=params)(
        moving, fixed, codes, from_left, from_right
    )
    lower, upper = neighbours(slabs, "px")
    peers = (lax.axis_size("px"), lax.axis_size("py"))

    def space(*lead, kind=f32):
        return pltpu.VMEM((*lead, blocks, rows + 2 * HALO, LANES), kind)

    return pl.pallas_call(
        functools.partial(gradient, peers),
        out_shape=jax.ShapeDtypeStruct((3, planes, rows, cols), jnp.bfloat16),
        scratch_shapes=[
            space(planes + 2),
            space(planes + 2),
            space(planes + 4, kind=jnp.int32),
            space(planes),
            space(4, planes + 4),
            space(4, planes + 4),
            space(planes),
            space(planes + 1),
            space(3, planes + 4),
        ],
        compiler_params=params,
    )(moving, fixed, codes, from_left, from_right, lower, upper)


def solution(mesh):
    placed = P(None, "px", "py")
    return jax.shard_map(
        shards, mesh=mesh, in_specs=(placed,) * 3, out_specs=P(None, None, "px", "py"), check_vma=False
    )
```

```python
import functools

import jax
import jax.numpy as jnp
from jax import lax
from jax.experimental import pallas as pl
from jax.experimental.pallas import tpu as pltpu
from jax.sharding import PartitionSpec as P

LANES = 128
HALO = 8
FIXED_HALO = 4
CODE_HALO = 6
SLAB = HALO + CODE_HALO + FIXED_HALO
VMEM = 32 * 1024 * 1024
FULL_VMEM = 60 * 1024 * 1024

Z1, X1, Y1 = 0.25, 0.375, 0.625
Z0, X0, Y0 = 1.0 - Z1, 1.0 - X1, 1.0 - Y1


def roll(value, shift):
    return pltpu.roll(value, shift % LANES, 1)


def shifted(blocks, step, lane):
    if step == 0:
        return blocks
    rolled = [roll(block, -step) for block in blocks]
    count = len(blocks)
    if step > 0:
        return [jnp.where(lane < LANES - step, rolled[b], rolled[(b + 1) % count]) for b in range(count)]
    return [jnp.where(lane >= -step, rolled[b], rolled[(b - 1) % count]) for b in range(count)]


def pack_columns(image_first, image_last, fixed_first, fixed_last, code_first, code_last, edge):
    planes, rows, _ = edge.shape
    lane = lax.broadcasted_iota(jnp.int32, (rows, LANES), 1)

    def ring(z, first, last):
        return jnp.where(lane < LANES // 2, first[z], last[z]).astype(jnp.float32)

    for z in range(planes):
        code = roll(ring(z, code_first, code_last), 2 * HALO)
        target = ring(z, fixed_first, fixed_last)
        packed = ring(z, image_first, image_last)
        packed = jnp.where((lane >= HALO) & (lane < 3 * HALO), code, packed)
        edge[z] = jnp.where((lane >= 3 * HALO) & (lane < 5 * HALO), roll(target, 4 * HALO), packed)


def merged_edge(pair, across, z, lane, even):
    left = (lane >= LANES - HALO) | ((lane >= HALO) & (lane < 2 * HALO)) | ((lane >= 3 * HALO) & (lane < 4 * HALO))
    return jnp.where(left != even, pair[z], across[z])


def pack_rows(moving, fixed, codes, pair, across):
    planes, rows, cols = moving.shape

    def pack(first, last):
        for z in range(planes):
            for b in range(cols // LANES):
                at = slice(b * LANES, (b + 1) * LANES)
                code = codes[z, :, at].astype(jnp.float32)
                target = fixed[z, :, at].astype(jnp.float32)
                row = b * SLAB
                first[z, row : row + HALO] = moving[z, :HALO, at]
                first[z, row + HALO : row + HALO + CODE_HALO] = code[:CODE_HALO]
                first[z, row + HALO + CODE_HALO : row + SLAB] = target[:FIXED_HALO]
                last[z, row : row + HALO] = moving[z, rows - HALO :, at]
                last[z, row + HALO : row + HALO + CODE_HALO] = code[rows - CODE_HALO :]
                last[z, row + HALO + CODE_HALO : row + SLAB] = target[rows - FIXED_HALO :]

    even = lax.axis_index("px") % 2 == 0
    pl.when(even)(functools.partial(pack, across, pair))
    pl.when(jnp.logical_not(even))(functools.partial(pack, pair, across))


def pack_corners(pair_edge, across_edge, pair_in, across_in, pair, across):
    planes, rows, _ = pair_edge.shape
    lane = lax.broadcasted_iota(jnp.int32, (rows, LANES), 1)
    even_y = lax.axis_index("py") % 2 == 0
    at = slice(pair.shape[1] - HALO, pair.shape[1])

    def corners(first, last):
        for z in range(planes):
            edge = merged_edge(pair_edge, across_edge, z, lane, even_y)
            first[z, at] = edge[:HALO]
            last[z, at] = edge[rows - HALO :]

    even = lax.axis_index("px") % 2 == 0
    pl.when(even)(functools.partial(corners, across, pair))
    pl.when(jnp.logical_not(even))(functools.partial(corners, pair, across))


def gradient(
    peers, moving, fixed, codes, pair_edge, across_edge, pair, across, out, image, first, code, target, table, parts, last, carried, raw
):
    planes, rows, cols = moving.shape
    inner = cols // LANES
    blocks = inner + 1
    f32 = jnp.float32
    lane = lax.broadcasted_iota(jnp.int32, (8, LANES), 1)
    row_at = lax.broadcasted_iota(jnp.int32, (8, LANES), 0)
    at_x, at_y = lax.axis_index("px"), lax.axis_index("py")
    least = jnp.where(at_x > 0, -HALO, 0)
    most = jnp.where(at_x < peers[0] - 1, rows + HALO, rows)
    has_left = (at_y > 0).astype(f32)
    has_right = (at_y < peers[1] - 1).astype(f32)
    ring_valid = jnp.where(lane < LANES // 2, has_right, has_left)

    def inside(value, x, b):
        if x < 0 or x + 8 > rows:
            value = jnp.where((row_at + x >= least) & (row_at + x < most), value, 0.0)
        if isinstance(b, int):
            return value * ring_valid if b == inner else value
        return value * jnp.where(b == inner, ring_valid, 1.0)

    def group(x):
        return slice(x + HALO, x + HALO + 8)

    zeros = jnp.zeros((blocks, 32, LANES), f32)
    for ref, spots in ((image, (0, planes + 1)), (first, (0, planes + 1))):
        for spot in spots:
            ref[spot] = zeros
    for o in range(4):
        for spot in (0, planes + 2):
            table[o, spot] = zeros
        for spot in (0, 1, planes + 2, planes + 3):
            parts[o, spot] = zeros
            if o < 3:
                raw[o, spot] = zeros

    own = slice(HALO, HALO + rows)
    wide_lane = lax.broadcasted_iota(jnp.int32, (rows, LANES), 1)

    def place_own(z, _):
        for b in range(inner):
            at = slice(b * LANES, (b + 1) * LANES)
            image[z + 1, b, own] = moving[z, :, at]
            code[z + 2, b, own] = codes[z, :, at]
            target[z, b, own] = fixed[z, :, at].astype(f32)
        place_edge(z, own, merged_edge(pair_edge, across_edge, z, wide_lane, at_y % 2 == 0))
        return 0

    def place_edge(z, at, edge):
        image[z + 1, inner, at] = edge
        code[z + 2, inner, at] = roll(edge, -2 * HALO).astype(jnp.int32)
        target[z, inner, at] = roll(edge, -4 * HALO)

    def place_rows(lower, upper):
        end = HALO + rows

        def plane(z, _):
            for b in range(inner):
                row = b * SLAB
                a = row + HALO
                c = a + CODE_HALO
                d = c + FIXED_HALO
                image[z + 1, b, 0:HALO] = lower[z, row:a]
                code[z + 2, b, HALO - CODE_HALO : HALO] = lower[z, a:c].astype(jnp.int32)
                target[z, b, HALO - FIXED_HALO : HALO] = lower[z, c:d]
                image[z + 1, b, end : end + HALO] = upper[z, row:a]
                code[z + 2, b, end : end + CODE_HALO] = upper[z, a:c].astype(jnp.int32)
                target[z, b, end : end + FIXED_HALO] = upper[z, c:d]
            place_edge(z, slice(0, HALO), lower[z, inner * SLAB :])
            place_edge(z, slice(end, end + HALO), upper[z, inner * SLAB :])
            return 0

        lax.fori_loop(0, planes, plane, 0)

    lax.fori_loop(0, planes, place_own, 0)
    even = at_x % 2 == 0
    pl.when(even)(functools.partial(place_rows, across, pair))
    pl.when(jnp.logical_not(even))(functools.partial(place_rows, pair, across))

    def fill_table(source, starts):
        def plane(z, _):
            for x in starts:
                at, up = group(x), group(x + 1)
                sums = [
                    (Z0 * X0) * source[z, b, at]
                    + (Z0 * X1) * source[z, b, up]
                    + (Z1 * X0) * source[z + 1, b, at]
                    + (Z1 * X1) * source[z + 1, b, up]
                    for b in range(blocks)
                ]
                moved = {step: shifted(sums, step, lane) for step in range(-2, 3)}
                for o in range(4):
                    for b in range(blocks):
                        table[o, z + 1, b, at] = Y0 * moved[o - 2][b] + Y1 * moved[o - 1][b]
            return 0

        lax.fori_loop(0, planes + 1, plane, 0)

    def masks(value):
        return [(value & (1 << bit)) != 0 for bit in range(6)]

    def choose(options, low, high):
        return jnp.where(high, jnp.where(low, options[3], options[2]), jnp.where(low, options[1], options[0]))

    def pick(z, b, x, bits):
        together = len(bits)
        found = [[] for _ in bits]
        for p in range(together + 3):
            users = [j for j in range(together) if 0 <= p - j < 4]
            lines = [[] for _ in bits]
            for ox in range(4):
                at = group(x + ox - 2)
                options = [table[oy, z + p, b, at] for oy in range(4)]
                for j in users:
                    lines[j].append(choose(options, bits[j][0], bits[j][1]))
            for j in users:
                found[j].append(choose(lines[j], bits[j][2], bits[j][3]))
        return [choose(found[j], bits[j][4], bits[j][5]) for j in range(together)]

    fill_table(image, (-8, 0, 8, 15))

    def first_planes(turn, _):
        z, b = 0, turn
        for x in (-6, 2, 6, 14):
            values = pick(z, b, x, [masks(code[z + j + 2, b, group(x)]) for j in range(planes)])
            for j, value in enumerate(values):
                first[z + j + 1, b, group(x)] = inside(value, x, b)
        return 0

    lax.fori_loop(0, blocks, first_planes, 0)

    fill_table(first, (-6, 2, 10, 13))

    def second_planes(turn, _):
        z, b = 0, turn
        for x in (-4, 4, 12):
            at = group(x)
            spots = [code[z + j + 2, b, at] for j in range(planes)]
            values = pick(z, b, x, [masks(spot) for spot in spots])
            for j, (spot, value) in enumerate(zip(spots, values)):
                value = inside(value - target[z + j, b, at], x, b)
                last[z + j, b, at] = value
                along = spot & 3
                for o in range(4):
                    parts[o, z + j + 2, b, at] = jnp.where(along == o, value, 0.0)
                code[z + j + 2, b, at] = lax.shift_right_logical(spot, 2)
        return 0

    lax.fori_loop(0, blocks, second_planes, 0)

    def land_planes(turn, _):
        z = turn * 3
        for b in range(blocks):
            for x in (-3, 5, 10):
                sums = [[None] * 4 for _ in range(3)]
                for p in range(3 + 3):
                    for ox in range(4):
                        at = group(x + 2 - ox)
                        spot = code[z + p, b, at]
                        values = [parts[oy, z + p, b, at] for oy in range(4)]
                        for j in range(3):
                            oz = j + 3 - p
                            if not 0 <= oz < 4:
                                continue
                            here = spot == oz * 4 + ox
                            for oy in range(4):
                                term = jnp.where(here, values[oy], 0.0)
                                sums[j][oy] = term if sums[j][oy] is None else sums[j][oy] + term
                for j in range(3):
                    for oy in range(4):
                        table[oy, z + j, b, group(x)] = sums[j][oy]
        return 0

    lax.fori_loop(0, (planes + 1) // 3, land_planes, 0)

    def carry_plane(z, _):
        for x in (-3, 5, 10):
            landed = [[table[oy, z, b, group(x)] for b in range(blocks)] for oy in range(4)]
            total = None
            for step in range(-2, 3):
                low, high = step + 2, step + 1
                terms = []
                for b in range(blocks):
                    term = Y0 * landed[low][b] if low < 4 else None
                    if high >= 0:
                        more = Y1 * landed[high][b]
                        term = more if term is None else term + more
                    terms.append(term)
                terms = shifted(terms, -step, lane)
                total = terms if total is None else [s + t for s, t in zip(total, terms)]
            for b in range(blocks):
                carried[z, b, group(x)] = total[b]
        return 0

    lax.fori_loop(0, planes + 1, carry_plane, 0)

    def raw_plane(z, _):
        for x in (-2, 6, 10):
            at, below, above = group(x), group(x - 1), group(x + 1)
            slope_one = [first[z + 1, b, at] for b in range(blocks)]
            slope_zero = [image[z + 1, b, at] for b in range(blocks)]
            slope_one = [s - t for s, t in zip(shifted(slope_one, 1, lane), shifted(slope_one, -1, lane))]
            slope_zero = [s - t for s, t in zip(shifted(slope_zero, 1, lane), shifted(slope_zero, -1, lane))]
            for b in range(blocks):
                one = inside(last[z, b, at], x, b)
                two = (
                    (Z0 * X0) * carried[z + 1, b, at]
                    + (Z0 * X1) * carried[z + 1, b, below]
                    + (Z1 * X0) * carried[z, b, at]
                    + (Z1 * X1) * carried[z, b, below]
                )
                two = inside(two, x, b)
                raw[0, z + 2, b, at] = one * (first[z + 2, b, at] - first[z, b, at]) + two * (image[z + 2, b, at] - image[z, b, at])
                raw[1, z + 2, b, at] = one * (first[z + 1, b, above] - first[z + 1, b, below]) + two * (
                    image[z + 1, b, above] - image[z + 1, b, below]
                )
                raw[2, z + 2, b, at] = one * slope_one[b] + two * slope_zero[b]
        return 0

    lax.fori_loop(0, planes, raw_plane, 0)

    def taps(a, b, c, d, e):
        return (a + e) + 4.0 * (b + d) + 6.0 * c

    def rows_plane(z, _):
        for k in range(3):
            for b in range(blocks):
                for x in range(0, rows, 8):
                    table[k, z, b, group(x)] = taps(*[raw[k, z, b, group(x + s)] for s in range(-2, 3)])
        return 0

    lax.fori_loop(0, planes + 4, rows_plane, 0)

    scale = -0.5 / 4096.0

    def out_plane(z, _):
        for k in range(3):
            halves = []
            for x in range(0, rows, 8):
                values = [taps(*[table[k, z + s, b, group(x)] for s in range(5)]) for b in range(blocks)]
                moved = [shifted(values, step, lane) for step in range(-2, 3)]
                halves.append([taps(*[m[b] for m in moved]) * scale for b in range(inner)])
            for b in range(inner):
                both = jnp.concatenate([half[b] for half in halves], axis=0)
                out[k, z, :, b * LANES : (b + 1) * LANES] = both.astype(out.dtype)
        return 0

    lax.fori_loop(0, planes, out_plane, 0)


def swapped(pair, across, axis):
    count = lax.axis_size(axis)
    ends = [(i, i + 1) for i in range(1, count - 1, 2)]
    pair = lax.ppermute(pair, axis, [(i, i ^ 1) for i in range(count)])
    return pair, lax.ppermute(across, axis, ends + [(j, i) for i, j in ends])


def shards(moving, fixed, codes):
    planes, rows, cols = moving.shape
    blocks = cols // LANES + 1
    f32 = jnp.float32
    params = pltpu.CompilerParams(vmem_limit_bytes=FULL_VMEM)

    def column(b):
        return pl.BlockSpec((planes, rows, LANES), lambda i: (0, 0, b))

    edge = pl.pallas_call(
        pack_columns,
        grid=(1,),
        in_specs=[column(0), column(blocks - 2)] * 3,
        out_specs=column(0),
        out_shape=jax.ShapeDtypeStruct((planes, rows, LANES), f32),
        compiler_params=params,
    )(moving, moving, fixed, fixed, codes, codes)
    edges = swapped(edge, edge, "py")
    slab = jax.ShapeDtypeStruct((planes, (blocks - 1) * SLAB + HALO, LANES), f32)
    params = pltpu.CompilerParams(vmem_limit_bytes=VMEM)
    slabs = pl.pallas_call(
        pack_rows,
        out_shape=(slab, slab),
        cost_estimate=pl.CostEstimate(flops=2**20, bytes_accessed=3 * 2**20, transcendentals=0),
        compiler_params=params,
    )(moving, fixed, codes)
    slabs = pl.pallas_call(
        pack_corners,
        out_shape=(slab, slab),
        input_output_aliases={2: 0, 3: 1},
        compiler_params=params,
    )(*edges, *slabs)
    slabs = swapped(*slabs, "px")
    peers = (lax.axis_size("px"), lax.axis_size("py"))

    def space(*lead, kind=f32):
        return pltpu.VMEM((*lead, blocks, rows + 2 * HALO, LANES), kind)

    return pl.pallas_call(
        functools.partial(gradient, peers),
        out_shape=jax.ShapeDtypeStruct((3, planes, rows, cols), jnp.bfloat16),
        scratch_shapes=[
            space(planes + 2),
            space(planes + 2),
            space(planes + 4, kind=jnp.int32),
            space(planes),
            space(4, planes + 4),
            space(4, planes + 4),
            space(planes),
            space(planes + 1),
            space(3, planes + 4),
        ],
        compiler_params=params,
    )(moving, fixed, codes, *edges, *slabs)


def solution(mesh):
    placed = P(None, "px", "py")
    return jax.shard_map(
        shards, mesh=mesh, in_specs=(placed,) * 3, out_specs=P(None, None, "px", "py"), check_vma=False
    )
```

```python
import functools

import jax
import jax.numpy as jnp
from jax import lax
from jax.experimental import pallas as pl
from jax.experimental.pallas import tpu as pltpu
from jax.sharding import PartitionSpec as P

LANES = 128
HALO = 8
FIXED_HALO = 4
CODE_HALO = 6
SLAB = HALO + CODE_HALO + FIXED_HALO
VMEM = 32 * 1024 * 1024
FULL_VMEM = 60 * 1024 * 1024

Z1, X1, Y1 = 0.25, 0.375, 0.625
Z0, X0, Y0 = 1.0 - Z1, 1.0 - X1, 1.0 - Y1


def roll(value, shift):
    return pltpu.roll(value, shift % LANES, 1)


def shifted(blocks, step, lane):
    if step == 0:
        return blocks
    rolled = [roll(block, -step) for block in blocks]
    count = len(blocks)
    if step > 0:
        return [jnp.where(lane < LANES - step, rolled[b], rolled[(b + 1) % count]) for b in range(count)]
    return [jnp.where(lane >= -step, rolled[b], rolled[(b - 1) % count]) for b in range(count)]


def pack_columns(image_first, image_last, fixed_first, fixed_last, code_first, code_last, edge):
    planes, rows, _ = edge.shape
    lane = lax.broadcasted_iota(jnp.int32, (rows, LANES), 1)

    def ring(z, first, last):
        return jnp.where(lane < LANES // 2, first[z], last[z]).astype(jnp.float32)

    for z in range(planes):
        code = roll(ring(z, code_first, code_last), 2 * HALO)
        target = ring(z, fixed_first, fixed_last)
        packed = ring(z, image_first, image_last)
        packed = jnp.where((lane >= HALO) & (lane < 3 * HALO), code, packed)
        edge[z] = jnp.where((lane >= 3 * HALO) & (lane < 5 * HALO), roll(target, 4 * HALO), packed)


def merged_edge(pair, across, z, lane, even):
    left = (lane >= LANES - HALO) | ((lane >= HALO) & (lane < 2 * HALO)) | ((lane >= 3 * HALO) & (lane < 4 * HALO))
    return jnp.where(left != even, pair[z], across[z])


def pack_rows(moving, fixed, codes, pair, across, image, code_at, target_at):
    planes, rows, cols = moving.shape
    own = slice(HALO, HALO + rows)
    for z in range(planes):
        for b in range(cols // LANES):
            at = slice(b * LANES, (b + 1) * LANES)
            image[z + 1, b, own] = moving[z, :, at]
            code_at[z + 2, b, own] = codes[z, :, at]
            target_at[z, b, own] = fixed[z, :, at].astype(jnp.float32)

    def pack(first, last):
        for z in range(planes):
            for b in range(cols // LANES):
                at = slice(b * LANES, (b + 1) * LANES)
                code = codes[z, :, at].astype(jnp.float32)
                target = fixed[z, :, at].astype(jnp.float32)
                row = b * SLAB
                first[z, row : row + HALO] = moving[z, :HALO, at]
                first[z, row + HALO : row + HALO + CODE_HALO] = code[:CODE_HALO]
                first[z, row + HALO + CODE_HALO : row + SLAB] = target[:FIXED_HALO]
                last[z, row : row + HALO] = moving[z, rows - HALO :, at]
                last[z, row + HALO : row + HALO + CODE_HALO] = code[rows - CODE_HALO :]
                last[z, row + HALO + CODE_HALO : row + SLAB] = target[rows - FIXED_HALO :]

    even = lax.axis_index("px") % 2 == 0
    pl.when(even)(functools.partial(pack, across, pair))
    pl.when(jnp.logical_not(even))(functools.partial(pack, pair, across))


def pack_corners(pair_edge, across_edge, pair_in, across_in, pair, across):
    planes, rows, _ = pair_edge.shape
    lane = lax.broadcasted_iota(jnp.int32, (rows, LANES), 1)
    even_y = lax.axis_index("py") % 2 == 0
    at = slice(pair.shape[1] - HALO, pair.shape[1])

    def corners(first, last):
        for z in range(planes):
            edge = merged_edge(pair_edge, across_edge, z, lane, even_y)
            first[z, at] = edge[:HALO]
            last[z, at] = edge[rows - HALO :]

    even = lax.axis_index("px") % 2 == 0
    pl.when(even)(functools.partial(corners, across, pair))
    pl.when(jnp.logical_not(even))(functools.partial(corners, pair, across))


class Stages:
    pass


def stages(peers, planes, rows, inner, held):
    image, first, code, target, last, table, second, parts, landed = held
    blocks = inner + 1
    f32 = jnp.float32
    lane = lax.broadcasted_iota(jnp.int32, (8, LANES), 1)
    row_at = lax.broadcasted_iota(jnp.int32, (8, LANES), 0)
    at_x, at_y = lax.axis_index("px"), lax.axis_index("py")
    least = jnp.where(at_x > 0, -HALO, 0)
    most = jnp.where(at_x < peers[0] - 1, rows + HALO, rows)
    has_left = (at_y > 0).astype(f32)
    has_right = (at_y < peers[1] - 1).astype(f32)
    ring_valid = jnp.where(lane < LANES // 2, has_right, has_left)

    def inside(value, x, b):
        if x < 0 or x + 8 > rows:
            value = jnp.where((row_at + x >= least) & (row_at + x < most), value, 0.0)
        if isinstance(b, int):
            return value * ring_valid if b == inner else value
        return value * jnp.where(b == inner, ring_valid, 1.0)

    def group(x):
        return slice(x + HALO, x + HALO + 8)

    def clear():
        zeros = jnp.zeros((blocks, 32, LANES), f32)
        for ref, spots in ((image, (0, planes + 1)), (first, (0, planes + 1))):
            for spot in spots:
                ref[spot] = zeros
        for o in range(4):
            for spot in (0, planes + 2):
                table[o, spot] = zeros
                second[o, spot] = zeros
            for spot in (0, 1, planes + 2, planes + 3):
                parts[o, spot] = zeros

    own = slice(HALO, HALO + rows)
    wide_lane = lax.broadcasted_iota(jnp.int32, (rows, LANES), 1)

    def place_edge(z, at, edge):
        image[z + 1, inner, at] = edge
        code[z + 2, inner, at] = roll(edge, -2 * HALO).astype(jnp.int32)
        target[z, inner, at] = roll(edge, -4 * HALO)

    def place_inner(pair_edge, across_edge):
        for z in range(planes):
            place_edge(z, own, merged_edge(pair_edge, across_edge, z, wide_lane, at_y % 2 == 0))

    def place_outer(pair, across):
        def place_rows(lower, upper):
            end = HALO + rows

            def plane(z, _):
                for b in range(inner):
                    row = b * SLAB
                    a = row + HALO
                    c = a + CODE_HALO
                    d = c + FIXED_HALO
                    image[z + 1, b, 0:HALO] = lower[z, row:a]
                    code[z + 2, b, HALO - CODE_HALO : HALO] = lower[z, a:c].astype(jnp.int32)
                    target[z, b, HALO - FIXED_HALO : HALO] = lower[z, c:d]
                    image[z + 1, b, end : end + HALO] = upper[z, row:a]
                    code[z + 2, b, end : end + CODE_HALO] = upper[z, a:c].astype(jnp.int32)
                    target[z, b, end : end + FIXED_HALO] = upper[z, c:d]
                place_edge(z, slice(0, HALO), lower[z, inner * SLAB :])
                place_edge(z, slice(end, end + HALO), upper[z, inner * SLAB :])
                return 0

            lax.fori_loop(0, planes, plane, 0)

        even = at_x % 2 == 0
        pl.when(even)(functools.partial(place_rows, across, pair))
        pl.when(jnp.logical_not(even))(functools.partial(place_rows, pair, across))

    def fill_table(source, table, starts):
        def plane(z, _):
            for x in starts:
                at, up = group(x), group(x + 1)
                sums = [
                    (Z0 * X0) * source[z, b, at]
                    + (Z0 * X1) * source[z, b, up]
                    + (Z1 * X0) * source[z + 1, b, at]
                    + (Z1 * X1) * source[z + 1, b, up]
                    for b in range(blocks)
                ]
                moved = {step: shifted(sums, step, lane) for step in range(-2, 3)}
                for o in range(4):
                    for b in range(blocks):
                        table[o, z + 1, b, at] = Y0 * moved[o - 2][b] + Y1 * moved[o - 1][b]
            return 0

        lax.fori_loop(0, planes + 1, plane, 0)

    def masks(value):
        return [(value & (1 << bit)) != 0 for bit in range(6)]

    def choose(options, low, high):
        return jnp.where(high, jnp.where(low, options[3], options[2]), jnp.where(low, options[1], options[0]))

    def pick(table, z, b, x, bits):
        together = len(bits)
        found = [[] for _ in bits]
        for p in range(together + 3):
            users = [j for j in range(together) if 0 <= p - j < 4]
            lines = [[] for _ in bits]
            for ox in range(4):
                at = group(x + ox - 2)
                options = [table[oy, z + p, b, at] for oy in range(4)]
                for j in users:
                    lines[j].append(choose(options, bits[j][0], bits[j][1]))
            for j in users:
                found[j].append(choose(lines[j], bits[j][2], bits[j][3]))
        return [choose(found[j], bits[j][4], bits[j][5]) for j in range(together)]

    def transport_once(starts):
        def first_planes(turn, _):
            z, b = 0, turn
            for x in starts:
                values = pick(table, z, b, x, [masks(code[z + j + 2, b, group(x)]) for j in range(planes)])
                for j, value in enumerate(values):
                    first[z + j + 1, b, group(x)] = inside(value, x, b)
            return 0

        lax.fori_loop(0, blocks, first_planes, 0)

    def transport_twice(starts):
        def second_planes(turn, _):
            z, b = 0, turn
            for x in starts:
                at = group(x)
                spots = [code[z + j + 2, b, at] for j in range(planes)]
                values = pick(second, z, b, x, [masks(spot) for spot in spots])
                for j, (spot, value) in enumerate(zip(spots, values)):
                    value = inside(value - target[z + j, b, at], x, b)
                    last[z + j, b, at] = value
                    along = spot & 3
                    for o in range(4):
                        parts[o, z + j + 2, b, at] = jnp.where(along == o, value, 0.0)
                    code[z + j + 2, b, at] = lax.shift_right_logical(spot, 2)
            return 0

        lax.fori_loop(0, blocks, second_planes, 0)

    def land(starts):
        def land_planes(turn, _):
            z = turn * 3
            for b in range(blocks):
                for x in starts:
                    sums = [[None] * 4 for _ in range(3)]
                    for p in range(3 + 3):
                        for ox in range(4):
                            at = group(x + 2 - ox)
                            spot = code[z + p, b, at]
                            values = [parts[oy, z + p, b, at] for oy in range(4)]
                            for j in range(3):
                                oz = j + 3 - p
                                if not 0 <= oz < 4:
                                    continue
                                here = spot == oz * 4 + ox
                                for oy in range(4):
                                    term = jnp.where(here, values[oy], 0.0)
                                    sums[j][oy] = term if sums[j][oy] is None else sums[j][oy] + term
                    for j in range(3):
                        for oy in range(4):
                            landed[oy, z + j, b, group(x)] = sums[j][oy]
            return 0

        lax.fori_loop(0, (planes + 1) // 3, land_planes, 0)

    def finish(out, carried, raw):
        for k in range(3):
            for spot in (0, 1, planes + 2, planes + 3):
                raw[k, spot] = jnp.zeros((blocks, rows + 2 * HALO, LANES), f32)

        def carry_plane(z, _):
            for x in (-3, 5, 10):
                found = [[landed[oy, z, b, group(x)] for b in range(blocks)] for oy in range(4)]
                total = None
                for step in range(-2, 3):
                    low, high = step + 2, step + 1
                    terms = []
                    for b in range(blocks):
                        term = Y0 * found[low][b] if low < 4 else None
                        if high >= 0:
                            more = Y1 * found[high][b]
                            term = more if term is None else term + more
                        terms.append(term)
                    terms = shifted(terms, -step, lane)
                    total = terms if total is None else [s + t for s, t in zip(total, terms)]
                for b in range(blocks):
                    carried[z, b, group(x)] = total[b]
            return 0

        lax.fori_loop(0, planes + 1, carry_plane, 0)

        def raw_plane(z, _):
            for x in (-2, 6, 10):
                at, below, above = group(x), group(x - 1), group(x + 1)
                slope_one = [first[z + 1, b, at] for b in range(blocks)]
                slope_zero = [image[z + 1, b, at] for b in range(blocks)]
                slope_one = [s - t for s, t in zip(shifted(slope_one, 1, lane), shifted(slope_one, -1, lane))]
                slope_zero = [s - t for s, t in zip(shifted(slope_zero, 1, lane), shifted(slope_zero, -1, lane))]
                for b in range(blocks):
                    one = inside(last[z, b, at], x, b)
                    two = (
                        (Z0 * X0) * carried[z + 1, b, at]
                        + (Z0 * X1) * carried[z + 1, b, below]
                        + (Z1 * X0) * carried[z, b, at]
                        + (Z1 * X1) * carried[z, b, below]
                    )
                    two = inside(two, x, b)
                    raw[0, z + 2, b, at] = one * (first[z + 2, b, at] - first[z, b, at]) + two * (image[z + 2, b, at] - image[z, b, at])
                    raw[1, z + 2, b, at] = one * (first[z + 1, b, above] - first[z + 1, b, below]) + two * (
                        image[z + 1, b, above] - image[z + 1, b, below]
                    )
                    raw[2, z + 2, b, at] = one * slope_one[b] + two * slope_zero[b]
            return 0

        lax.fori_loop(0, planes, raw_plane, 0)

        def taps(a, b, c, d, e):
            return (a + e) + 4.0 * (b + d) + 6.0 * c

        def rows_plane(z, _):
            for k in range(3):
                for b in range(blocks):
                    for x in range(0, rows, 8):
                        table[k, z, b, group(x)] = taps(*[raw[k, z, b, group(x + s)] for s in range(-2, 3)])
            return 0

        lax.fori_loop(0, planes + 4, rows_plane, 0)

        scale = -0.5 / 4096.0

        def out_plane(z, _):
            for k in range(3):
                halves = []
                for x in range(0, rows, 8):
                    values = [taps(*[table[k, z + s, b, group(x)] for s in range(5)]) for b in range(blocks)]
                    moved = [shifted(values, step, lane) for step in range(-2, 3)]
                    halves.append([taps(*[m[b] for m in moved]) * scale for b in range(inner)])
                for b in range(inner):
                    both = jnp.concatenate([half[b] for half in halves], axis=0)
                    out[k, z, :, b * LANES : (b + 1) * LANES] = both.astype(out.dtype)
            return 0

        lax.fori_loop(0, planes, out_plane, 0)

    made = Stages()
    made.clear, made.place_inner, made.place_outer, made.fill_table = clear, place_inner, place_outer, fill_table
    made.transport_once, made.transport_twice, made.land, made.finish = transport_once, transport_twice, land, finish
    return made


def inner_cells(peers, planes, rows, inner, pair_edge, across_edge, image_in, code_in, target_in, *held):
    image, first, code, target, last, table, second, parts, landed = held
    run = stages(peers, planes, rows, inner, held)
    run.clear()
    run.place_inner(pair_edge, across_edge)
    run.fill_table(image, table, (0, 7))
    run.transport_once((2, 6))
    run.fill_table(first, second, (2, 5))
    run.transport_twice((4,))
    run.land((5,))


def outer_cells(peers, pair, across, *refs):
    out, held, (carried, raw) = refs[9], refs[10:19], refs[19:]
    planes, rows, cols = out.shape[1:]
    image, first, code, target, last, table, second, parts, landed = held
    run = stages(peers, planes, rows, cols // LANES, held)
    run.place_outer(pair, across)
    run.fill_table(image, table, (-8, 15))
    run.transport_once((-6, 14))
    run.fill_table(first, second, (-6, 13))
    run.transport_twice((-4, 12))
    run.land((-3, 10))
    run.finish(out, carried, raw)


def swapped(pair, across, axis):
    count = lax.axis_size(axis)
    ends = [(i, i + 1) for i in range(1, count - 1, 2)]
    pair = lax.ppermute(pair, axis, [(i, i ^ 1) for i in range(count)])
    return pair, lax.ppermute(across, axis, ends + [(j, i) for i, j in ends])


def shards(moving, fixed, codes):
    planes, rows, cols = moving.shape
    blocks = cols // LANES + 1
    f32 = jnp.float32
    params = pltpu.CompilerParams(vmem_limit_bytes=FULL_VMEM)

    def column(b):
        return pl.BlockSpec((planes, rows, LANES), lambda i: (0, 0, b))

    edge = pl.pallas_call(
        pack_columns,
        grid=(1,),
        in_specs=[column(0), column(blocks - 2)] * 3,
        out_specs=column(0),
        out_shape=jax.ShapeDtypeStruct((planes, rows, LANES), f32),
        compiler_params=params,
    )(moving, moving, fixed, fixed, codes, codes)
    edges = swapped(edge, edge, "py")
    slab = jax.ShapeDtypeStruct((planes, (blocks - 1) * SLAB + HALO, LANES), f32)
    params = pltpu.CompilerParams(vmem_limit_bytes=VMEM)

    def space(*lead, kind=f32):
        return jax.ShapeDtypeStruct((*lead, blocks, rows + 2 * HALO, LANES), kind)

    image, code, target = space(planes + 2), space(planes + 4, kind=jnp.int32), space(planes)
    *slabs, image, code, target = pl.pallas_call(
        pack_rows,
        out_shape=(slab, slab, image, code, target),
        cost_estimate=pl.CostEstimate(flops=2**20, bytes_accessed=3 * 2**20, transcendentals=0),
        compiler_params=params,
    )(moving, fixed, codes)
    slabs = pl.pallas_call(
        pack_corners,
        out_shape=(slab, slab),
        input_output_aliases={2: 0, 3: 1},
        compiler_params=params,
    )(*edges, *slabs)
    slabs = swapped(*slabs, "px")
    peers = (lax.axis_size("px"), lax.axis_size("py"))
    held = [
        space(planes + 2),
        space(planes + 2),
        space(planes + 4, kind=jnp.int32),
        space(planes),
        space(planes),
        space(4, planes + 4),
        space(4, planes + 3),
        space(4, planes + 4),
        space(4, planes + 1),
    ]
    held = pl.pallas_call(
        functools.partial(inner_cells, peers, planes, rows, blocks - 1),
        out_shape=held,
        input_output_aliases={2: 0, 3: 2, 4: 3},
        cost_estimate=pl.CostEstimate(flops=2**24, bytes_accessed=2**24, transcendentals=0),
        compiler_params=params,
    )(*edges, image, code, target)
    return pl.pallas_call(
        functools.partial(outer_cells, peers),
        out_shape=[jax.ShapeDtypeStruct((3, planes, rows, cols), jnp.bfloat16), *held],
        input_output_aliases={2 + i: 1 + i for i in range(len(held))},
        scratch_shapes=[pltpu.VMEM(a.shape, a.dtype) for a in (space(planes + 1), space(3, planes + 4))],
        compiler_params=params,
    )(*slabs, *held)[0]


def solution(mesh):
    placed = P(None, "px", "py")
    return jax.shard_map(
        shards, mesh=mesh, in_specs=(placed,) * 3, out_specs=P(None, None, "px", "py"), check_vma=False
    )
```

```python
import functools

import jax
import jax.numpy as jnp
from jax import lax
from jax.experimental import pallas as pl
from jax.experimental.pallas import tpu as pltpu
from jax.sharding import PartitionSpec as P

LANES = 128
HALO = 8
FIXED_HALO = 4
CODE_HALO = 6
SLAB = HALO + CODE_HALO + FIXED_HALO
VMEM = 32 * 1024 * 1024
PACK_VMEM = 8 * 1024 * 1024

Z1, X1, Y1 = 0.25, 0.375, 0.625
Z0, X0, Y0 = 1.0 - Z1, 1.0 - X1, 1.0 - Y1


def roll(value, shift):
    return pltpu.roll(value, shift % LANES, 1)


def shifted(blocks, step, lane):
    if step == 0:
        return blocks
    rolled = [roll(block, -step) for block in blocks]
    count = len(blocks)
    if step > 0:
        return [jnp.where(lane < LANES - step, rolled[b], rolled[(b + 1) % count]) for b in range(count)]
    return [jnp.where(lane >= -step, rolled[b], rolled[(b - 1) % count]) for b in range(count)]


def merged_edge(pair, across, z, lane, even):
    left = (lane >= LANES - HALO) | ((lane >= HALO) & (lane < 2 * HALO)) | ((lane >= 3 * HALO) & (lane < 4 * HALO))
    return jnp.where(left != even, pair[z], across[z])


def pack(moving, fixed, codes, edge, pair, across, image, code_at, target_at):
    planes, rows, cols = moving.shape
    own = slice(HALO, HALO + rows)
    lane = lax.broadcasted_iota(jnp.int32, (rows, LANES), 1)

    def ring(held, z):
        return jnp.where(lane < LANES // 2, held[z, :, :LANES], held[z, :, cols - LANES :]).astype(jnp.float32)

    for z in range(planes):
        code, target = roll(ring(codes, z), 2 * HALO), roll(ring(fixed, z), 4 * HALO)
        packed = jnp.where((lane >= HALO) & (lane < 3 * HALO), code, ring(moving, z))
        edge[z] = jnp.where((lane >= 3 * HALO) & (lane < 5 * HALO), target, packed)
        for b in range(cols // LANES):
            at = slice(b * LANES, (b + 1) * LANES)
            image[z + 1, b, own] = moving[z, :, at]
            code_at[z + 2, b, own] = codes[z, :, at]
            target_at[z, b, own] = fixed[z, :, at].astype(jnp.float32)

    def slabs(first, last):
        for z in range(planes):
            for b in range(cols // LANES):
                at = slice(b * LANES, (b + 1) * LANES)
                code = codes[z, :, at].astype(jnp.float32)
                target = fixed[z, :, at].astype(jnp.float32)
                row = b * SLAB
                first[z, row : row + HALO] = moving[z, :HALO, at]
                first[z, row + HALO : row + HALO + CODE_HALO] = code[:CODE_HALO]
                first[z, row + HALO + CODE_HALO : row + SLAB] = target[:FIXED_HALO]
                last[z, row : row + HALO] = moving[z, rows - HALO :, at]
                last[z, row + HALO : row + HALO + CODE_HALO] = code[rows - CODE_HALO :]
                last[z, row + HALO + CODE_HALO : row + SLAB] = target[rows - FIXED_HALO :]

    even = lax.axis_index("px") % 2 == 0
    pl.when(even)(functools.partial(slabs, across, pair))
    pl.when(jnp.logical_not(even))(functools.partial(slabs, pair, across))


def pack_corners(pair_edge, across_edge, pair, across):
    planes, rows, _ = pair_edge.shape
    lane = lax.broadcasted_iota(jnp.int32, (rows, LANES), 1)
    even_y = lax.axis_index("py") % 2 == 0

    def corners(first, last):
        for z in range(planes):
            edge = merged_edge(pair_edge, across_edge, z, lane, even_y)
            first[z] = edge[:HALO]
            last[z] = edge[rows - HALO :]

    even = lax.axis_index("px") % 2 == 0
    pl.when(even)(functools.partial(corners, across, pair))
    pl.when(jnp.logical_not(even))(functools.partial(corners, pair, across))


class Stages:
    pass


def stages(peers, planes, rows, inner, held):
    image, first, code, target, last, table, second, parts, landed = held
    blocks = inner + 1
    f32 = jnp.float32
    lane = lax.broadcasted_iota(jnp.int32, (8, LANES), 1)
    row_at = lax.broadcasted_iota(jnp.int32, (8, LANES), 0)
    at_x, at_y = lax.axis_index("px"), lax.axis_index("py")
    least = jnp.where(at_x > 0, -HALO, 0)
    most = jnp.where(at_x < peers[0] - 1, rows + HALO, rows)
    has_left = (at_y > 0).astype(f32)
    has_right = (at_y < peers[1] - 1).astype(f32)
    ring_valid = jnp.where(lane < LANES // 2, has_right, has_left)

    def inside(value, x, b):
        if x < 0 or x + 8 > rows:
            value = jnp.where((row_at + x >= least) & (row_at + x < most), value, 0.0)
        if isinstance(b, int):
            return value * ring_valid if b == inner else value
        return value * jnp.where(b == inner, ring_valid, 1.0)

    def group(x):
        return slice(x + HALO, x + HALO + 8)

    def clear():
        zeros = jnp.zeros((blocks, 32, LANES), f32)
        for ref, spots in ((image, (0, planes + 1)), (first, (0, planes + 1))):
            for spot in spots:
                ref[spot] = zeros
        for o in range(4):
            for spot in (0, planes + 2):
                table[o, spot] = zeros
                second[o, spot] = zeros
            for spot in (0, 1, planes + 2, planes + 3):
                parts[o, spot] = zeros

    own = slice(HALO, HALO + rows)
    wide_lane = lax.broadcasted_iota(jnp.int32, (rows, LANES), 1)

    def place_edge(z, at, edge, factor=1.0):
        image[z + 1, inner, at] = edge * factor
        code[z + 2, inner, at] = roll(edge, -2 * HALO).astype(jnp.int32)
        target[z, inner, at] = roll(edge, -4 * HALO)

    def place_inner(pair_edge, across_edge):
        for z in range(planes):
            place_edge(z, own, merged_edge(pair_edge, across_edge, z, wide_lane, at_y % 2 == 0))

    def place_outer(pair, across, pair_corner, across_corner):
        end = HALO + rows
        has_lower = (at_x > 0).astype(f32)
        has_upper = (at_x < peers[0] - 1).astype(f32)

        def place_rows(lower, upper, lower_corner, upper_corner):
            def plane(z, _):
                for b in range(inner):
                    row = b * SLAB
                    a = row + HALO
                    c = a + CODE_HALO
                    d = c + FIXED_HALO
                    image[z + 1, b, 0:HALO] = lower[z, row:a] * has_lower
                    code[z + 2, b, HALO - CODE_HALO : HALO] = lower[z, a:c].astype(jnp.int32)
                    target[z, b, HALO - FIXED_HALO : HALO] = lower[z, c:d]
                    image[z + 1, b, end : end + HALO] = upper[z, row:a] * has_upper
                    code[z + 2, b, end : end + CODE_HALO] = upper[z, a:c].astype(jnp.int32)
                    target[z, b, end : end + FIXED_HALO] = upper[z, c:d]
                place_edge(z, slice(0, HALO), lower_corner[z], has_lower)
                place_edge(z, slice(end, end + HALO), upper_corner[z], has_upper)
                return 0

            lax.fori_loop(0, planes, plane, 0)

        even = at_x % 2 == 0
        pl.when(even)(functools.partial(place_rows, across, pair, across_corner, pair_corner))
        pl.when(jnp.logical_not(even))(functools.partial(place_rows, pair, across, pair_corner, across_corner))

    def fill_table(source, table, starts):
        def plane(z, _):
            for x in starts:
                at, up = group(x), group(x + 1)
                sums = [
                    (Z0 * X0) * source[z, b, at]
                    + (Z0 * X1) * source[z, b, up]
                    + (Z1 * X0) * source[z + 1, b, at]
                    + (Z1 * X1) * source[z + 1, b, up]
                    for b in range(blocks)
                ]
                moved = {step: shifted(sums, step, lane) for step in range(-2, 3)}
                for o in range(4):
                    for b in range(blocks):
                        table[o, z + 1, b, at] = Y0 * moved[o - 2][b] + Y1 * moved[o - 1][b]
            return 0

        lax.fori_loop(0, planes + 1, plane, 0)

    def masks(value):
        return [(value & (1 << bit)) != 0 for bit in range(6)]

    def choose(options, low, high):
        return jnp.where(high, jnp.where(low, options[3], options[2]), jnp.where(low, options[1], options[0]))

    def pick(table, z, b, x, bits):
        together = len(bits)
        found = [[] for _ in bits]
        for p in range(together + 3):
            users = [j for j in range(together) if 0 <= p - j < 4]
            lines = [[] for _ in bits]
            for ox in range(4):
                at = group(x + ox - 2)
                options = [table[oy, z + p, b, at] for oy in range(4)]
                for j in users:
                    lines[j].append(choose(options, bits[j][0], bits[j][1]))
            for j in users:
                found[j].append(choose(lines[j], bits[j][2], bits[j][3]))
        return [choose(found[j], bits[j][4], bits[j][5]) for j in range(together)]

    def transport_once(starts):
        def first_planes(turn, _):
            z, b = 0, turn
            for x in starts:
                values = pick(table, z, b, x, [masks(code[z + j + 2, b, group(x)]) for j in range(planes)])
                for j, value in enumerate(values):
                    first[z + j + 1, b, group(x)] = inside(value, x, b)
            return 0

        lax.fori_loop(0, blocks, first_planes, 0)

    def transport_twice(starts):
        def second_planes(turn, _):
            z, b = 0, turn
            for x in starts:
                at = group(x)
                spots = [code[z + j + 2, b, at] for j in range(planes)]
                values = pick(second, z, b, x, [masks(spot) for spot in spots])
                for j, (spot, value) in enumerate(zip(spots, values)):
                    value = inside(value - target[z + j, b, at], x, b)
                    last[z + j, b, at] = value
                    along = spot & 3
                    for o in range(4):
                        parts[o, z + j + 2, b, at] = jnp.where(along == o, value, 0.0)
                    code[z + j + 2, b, at] = lax.shift_right_logical(spot, 2)
            return 0

        lax.fori_loop(0, blocks, second_planes, 0)

    def land(starts):
        def land_planes(turn, _):
            z = turn * 3
            for b in range(blocks):
                for x in starts:
                    sums = [[None] * 4 for _ in range(3)]
                    for p in range(3 + 3):
                        for ox in range(4):
                            at = group(x + 2 - ox)
                            spot = code[z + p, b, at]
                            values = [parts[oy, z + p, b, at] for oy in range(4)]
                            for j in range(3):
                                oz = j + 3 - p
                                if not 0 <= oz < 4:
                                    continue
                                here = spot == oz * 4 + ox
                                for oy in range(4):
                                    term = jnp.where(here, values[oy], 0.0)
                                    sums[j][oy] = term if sums[j][oy] is None else sums[j][oy] + term
                    for j in range(3):
                        for oy in range(4):
                            landed[oy, z + j, b, group(x)] = sums[j][oy]
            return 0

        lax.fori_loop(0, (planes + 1) // 3, land_planes, 0)

    def finish(out, carried, raw):
        for k in range(3):
            for spot in (0, 1, planes + 2, planes + 3):
                raw[k, spot] = jnp.zeros((blocks, rows + 2 * HALO, LANES), f32)

        def carry_plane(z, _):
            for x in (-3, 5, 10):
                found = [[landed[oy, z, b, group(x)] for b in range(blocks)] for oy in range(4)]
                total = None
                for step in range(-2, 3):
                    low, high = step + 2, step + 1
                    terms = []
                    for b in range(blocks):
                        term = Y0 * found[low][b] if low < 4 else None
                        if high >= 0:
                            more = Y1 * found[high][b]
                            term = more if term is None else term + more
                        terms.append(term)
                    terms = shifted(terms, -step, lane)
                    total = terms if total is None else [s + t for s, t in zip(total, terms)]
                for b in range(blocks):
                    carried[z, b, group(x)] = total[b]
            return 0

        lax.fori_loop(0, planes + 1, carry_plane, 0)

        def raw_plane(z, _):
            for x in (-2, 6, 10):
                at, below, above = group(x), group(x - 1), group(x + 1)
                slope_one = [first[z + 1, b, at] for b in range(blocks)]
                slope_zero = [image[z + 1, b, at] for b in range(blocks)]
                slope_one = [s - t for s, t in zip(shifted(slope_one, 1, lane), shifted(slope_one, -1, lane))]
                slope_zero = [s - t for s, t in zip(shifted(slope_zero, 1, lane), shifted(slope_zero, -1, lane))]
                for b in range(blocks):
                    one = inside(last[z, b, at], x, b)
                    two = (
                        (Z0 * X0) * carried[z + 1, b, at]
                        + (Z0 * X1) * carried[z + 1, b, below]
                        + (Z1 * X0) * carried[z, b, at]
                        + (Z1 * X1) * carried[z, b, below]
                    )
                    two = inside(two, x, b)
                    raw[0, z + 2, b, at] = one * (first[z + 2, b, at] - first[z, b, at]) + two * (image[z + 2, b, at] - image[z, b, at])
                    raw[1, z + 2, b, at] = one * (first[z + 1, b, above] - first[z + 1, b, below]) + two * (
                        image[z + 1, b, above] - image[z + 1, b, below]
                    )
                    raw[2, z + 2, b, at] = one * slope_one[b] + two * slope_zero[b]
            return 0

        lax.fori_loop(0, planes, raw_plane, 0)

        def taps(a, b, c, d, e):
            return (a + e) + 4.0 * (b + d) + 6.0 * c

        def rows_plane(z, _):
            for k in range(3):
                for b in range(blocks):
                    for x in range(0, rows, 8):
                        table[k, z, b, group(x)] = taps(*[raw[k, z, b, group(x + s)] for s in range(-2, 3)])
            return 0

        lax.fori_loop(0, planes + 4, rows_plane, 0)

        scale = -0.5 / 4096.0

        def out_plane(z, _):
            for k in range(3):
                halves = []
                for x in range(0, rows, 8):
                    values = [taps(*[table[k, z + s, b, group(x)] for s in range(5)]) for b in range(blocks)]
                    moved = [shifted(values, step, lane) for step in range(-2, 3)]
                    halves.append([taps(*[m[b] for m in moved]) * scale for b in range(inner)])
                for b in range(inner):
                    both = jnp.concatenate([half[b] for half in halves], axis=0)
                    out[k, z, :, b * LANES : (b + 1) * LANES] = both.astype(out.dtype)
            return 0

        lax.fori_loop(0, planes, out_plane, 0)

    made = Stages()
    made.clear, made.place_inner, made.place_outer, made.fill_table = clear, place_inner, place_outer, fill_table
    made.transport_once, made.transport_twice, made.land, made.finish = transport_once, transport_twice, land, finish
    return made


def inner_cells(peers, planes, rows, inner, pair_edge, across_edge, image_in, code_in, target_in, *held):
    image, first, code, target, last, table, second, parts, landed = held
    run = stages(peers, planes, rows, inner, held)
    run.clear()
    run.place_inner(pair_edge, across_edge)
    run.fill_table(image, table, (0, 7))
    run.transport_once((2, 6))
    run.fill_table(first, second, (2, 5))
    run.transport_twice((4,))
    run.land((5,))


def outer_cells(peers, pair, across, pair_corner, across_corner, *refs):
    out, held, (carried, raw) = refs[9], refs[10:19], refs[19:]
    planes, rows, cols = out.shape[1:]
    image, first, code, target, last, table, second, parts, landed = held
    run = stages(peers, planes, rows, cols // LANES, held)
    run.place_outer(pair, across, pair_corner, across_corner)
    run.fill_table(image, table, (-8, 15))
    run.transport_once((-6, 14))
    run.fill_table(first, second, (-6, 13))
    run.transport_twice((-4, 12))
    run.land((-3, 10))
    run.finish(out, carried, raw)


def swapped(pair, across, axis, ends):
    count = lax.axis_size(axis)
    rest = [(i, i + 1) for i in range(1, count - 1, 2)] + ([(0, count - 1)] if ends else [])
    pair = lax.ppermute(pair, axis, [(i, i ^ 1) for i in range(count)])
    return pair, lax.ppermute(across, axis, rest + [(j, i) for i, j in rest])


def shards(moving, fixed, codes):
    planes, rows, cols = moving.shape
    blocks = cols // LANES + 1
    f32 = jnp.float32
    params = pltpu.CompilerParams(vmem_limit_bytes=VMEM)
    slab = jax.ShapeDtypeStruct((planes, (blocks - 1) * SLAB, LANES), f32)
    corner = jax.ShapeDtypeStruct((planes, HALO, LANES), f32)

    def space(*lead, kind=f32):
        return jax.ShapeDtypeStruct((*lead, blocks, rows + 2 * HALO, LANES), kind)

    placed = (space(planes + 2), space(planes + 4, kind=jnp.int32), space(planes))
    edge, *slabs, image, code, target = pl.pallas_call(
        pack,
        out_shape=(jax.ShapeDtypeStruct((planes, rows, LANES), f32), slab, slab, *placed),
        compiler_params=pltpu.CompilerParams(vmem_limit_bytes=PACK_VMEM),
    )(moving, fixed, codes)
    edges = swapped(edge, edge, "py", False)
    slabs = swapped(*slabs, "px", True)
    corners = pl.pallas_call(
        pack_corners,
        out_shape=(corner, corner),
        cost_estimate=pl.CostEstimate(flops=2**24, bytes_accessed=2**24, transcendentals=0),
        compiler_params=params,
    )(*edges)
    corners = swapped(*corners, "px", True)
    peers = (lax.axis_size("px"), lax.axis_size("py"))

    held = [
        space(planes + 2),
        space(planes + 2),
        space(planes + 4, kind=jnp.int32),
        space(planes),
        space(planes),
        space(4, planes + 4),
        space(4, planes + 3),
        space(4, planes + 4),
        space(4, planes + 1),
    ]
    held = pl.pallas_call(
        functools.partial(inner_cells, peers, planes, rows, blocks - 1),
        out_shape=held,
        input_output_aliases={2: 0, 3: 2, 4: 3},
        cost_estimate=pl.CostEstimate(flops=2**24, bytes_accessed=2**24, transcendentals=0),
        compiler_params=params,
    )(*edges, image, code, target)
    return pl.pallas_call(
        functools.partial(outer_cells, peers),
        out_shape=[jax.ShapeDtypeStruct((3, planes, rows, cols), jnp.bfloat16), *held],
        input_output_aliases={4 + i: 1 + i for i in range(len(held))},
        scratch_shapes=[pltpu.VMEM(a.shape, a.dtype) for a in (space(planes + 1), space(3, planes + 4))],
        compiler_params=params,
    )(*slabs, *corners, *held)[0]


def solution(mesh):
    placed = P(None, "px", "py")
    return jax.shard_map(
        shards, mesh=mesh, in_specs=(placed,) * 3, out_specs=P(None, None, "px", "py"), check_vma=False
    )
```

```python
import functools

import jax
import jax.numpy as jnp
from jax import lax
from jax.experimental import pallas as pl
from jax.experimental.pallas import tpu as pltpu
from jax.sharding import PartitionSpec as P

LANES = 128
HALO = 8
FIXED_HALO = 4
CODE_HALO = 6
SLAB = HALO + CODE_HALO + FIXED_HALO
VMEM = 32 * 1024 * 1024
PACK_VMEM = 8 * 1024 * 1024

Z1, X1, Y1 = 0.25, 0.375, 0.625
Z0, X0, Y0 = 1.0 - Z1, 1.0 - X1, 1.0 - Y1


def roll(value, shift):
    return pltpu.roll(value, shift % LANES, 1)


def shifted(blocks, step, lane):
    if step == 0:
        return blocks
    rolled = [roll(block, -step) for block in blocks]
    count = len(blocks)
    if step > 0:
        return [jnp.where(lane < LANES - step, rolled[b], rolled[(b + 1) % count]) for b in range(count)]
    return [jnp.where(lane >= -step, rolled[b], rolled[(b - 1) % count]) for b in range(count)]


def merged_edge(pair, across, z, lane, even):
    left = (lane >= LANES - HALO) | ((lane >= HALO) & (lane < 2 * HALO)) | ((lane >= 3 * HALO) & (lane < 4 * HALO))
    return jnp.where(left != even, pair[z], across[z])


def pack(moving, fixed, codes, edge, pair, across, image, code_at, target_at):
    planes, rows, cols = moving.shape
    own = slice(HALO, HALO + rows)
    lane = lax.broadcasted_iota(jnp.int32, (rows, LANES), 1)

    def ring(held, z):
        return jnp.where(lane < LANES // 2, held[z, :, :LANES], held[z, :, cols - LANES :]).astype(jnp.float32)

    for z in range(planes):
        code, target = roll(ring(codes, z), 2 * HALO), roll(ring(fixed, z), 4 * HALO)
        packed = jnp.where((lane >= HALO) & (lane < 3 * HALO), code, ring(moving, z))
        edge[z] = jnp.where((lane >= 3 * HALO) & (lane < 5 * HALO), target, packed)
        for b in range(cols // LANES):
            at = slice(b * LANES, (b + 1) * LANES)
            image[z + 1, b, own] = moving[z, :, at]
            code_at[z + 2, b, own] = codes[z, :, at]
            target_at[z, b, own] = fixed[z, :, at].astype(jnp.float32)

    def slabs(first, last):
        for z in range(planes):
            for b in range(cols // LANES):
                at = slice(b * LANES, (b + 1) * LANES)
                code = codes[z, :, at].astype(jnp.float32)
                target = fixed[z, :, at].astype(jnp.float32)
                row = b * SLAB
                first[z, row : row + HALO] = moving[z, :HALO, at]
                first[z, row + HALO : row + HALO + CODE_HALO] = code[:CODE_HALO]
                first[z, row + HALO + CODE_HALO : row + SLAB] = target[:FIXED_HALO]
                last[z, row : row + HALO] = moving[z, rows - HALO :, at]
                last[z, row + HALO : row + HALO + CODE_HALO] = code[rows - CODE_HALO :]
                last[z, row + HALO + CODE_HALO : row + SLAB] = target[rows - FIXED_HALO :]

    even = lax.axis_index("px") % 2 == 0
    pl.when(even)(functools.partial(slabs, across, pair))
    pl.when(jnp.logical_not(even))(functools.partial(slabs, pair, across))


def pack_corners(pair_edge, across_edge, pair, across):
    planes, rows, _ = pair_edge.shape
    lane = lax.broadcasted_iota(jnp.int32, (rows, LANES), 1)
    even_y = lax.axis_index("py") % 2 == 0

    def corners(first, last):
        for z in range(planes):
            edge = merged_edge(pair_edge, across_edge, z, lane, even_y)
            first[z] = edge[:HALO]
            last[z] = edge[rows - HALO :]

    even = lax.axis_index("px") % 2 == 0
    pl.when(even)(functools.partial(corners, across, pair))
    pl.when(jnp.logical_not(even))(functools.partial(corners, pair, across))


class Stages:
    pass


def stages(peers, planes, rows, inner, held):
    image, first, code, target, last, table, second, parts, landed = held
    blocks = inner + 1
    f32 = jnp.float32
    lane = lax.broadcasted_iota(jnp.int32, (8, LANES), 1)
    row_at = lax.broadcasted_iota(jnp.int32, (8, LANES), 0)
    at_x, at_y = lax.axis_index("px"), lax.axis_index("py")
    least = jnp.where(at_x > 0, -HALO, 0)
    most = jnp.where(at_x < peers[0] - 1, rows + HALO, rows)
    has_left = (at_y > 0).astype(f32)
    has_right = (at_y < peers[1] - 1).astype(f32)
    ring_valid = jnp.where(lane < LANES // 2, has_right, has_left)

    def inside(value, x, b):
        if x < 0 or x + 8 > rows:
            value = jnp.where((row_at + x >= least) & (row_at + x < most), value, 0.0)
        if isinstance(b, int):
            return value * ring_valid if b == inner else value
        return value * jnp.where(b == inner, ring_valid, 1.0)

    def group(x):
        return slice(x + HALO, x + HALO + 8)

    def clear():
        zeros = jnp.zeros((blocks, 32, LANES), f32)
        for ref, spots in ((image, (0, planes + 1)), (first, (0, planes + 1))):
            for spot in spots:
                ref[spot] = zeros
        for o in range(4):
            for spot in (0, planes + 2):
                table[o, spot] = zeros
                second[o, spot] = zeros
            for spot in (0, 1, planes + 2, planes + 3):
                parts[o, spot] = zeros

    own = slice(HALO, HALO + rows)
    wide_lane = lax.broadcasted_iota(jnp.int32, (rows, LANES), 1)

    def place_edge(z, at, edge, factor=1.0):
        image[z + 1, inner, at] = edge * factor
        code[z + 2, inner, at] = roll(edge, -2 * HALO).astype(jnp.int32)
        target[z, inner, at] = roll(edge, -4 * HALO)

    def place_inner(pair_edge, across_edge):
        for z in range(planes):
            place_edge(z, own, merged_edge(pair_edge, across_edge, z, wide_lane, at_y % 2 == 0))

    def place_outer(pair, across, pair_corner, across_corner):
        end = HALO + rows
        has_lower = (at_x > 0).astype(f32)
        has_upper = (at_x < peers[0] - 1).astype(f32)

        def place_rows(lower, upper, lower_corner, upper_corner):
            def plane(z, _):
                for b in range(inner):
                    row = b * SLAB
                    a = row + HALO
                    c = a + CODE_HALO
                    d = c + FIXED_HALO
                    image[z + 1, b, 0:HALO] = lower[z, row:a] * has_lower
                    code[z + 2, b, HALO - CODE_HALO : HALO] = lower[z, a:c].astype(jnp.int32)
                    target[z, b, HALO - FIXED_HALO : HALO] = lower[z, c:d]
                    image[z + 1, b, end : end + HALO] = upper[z, row:a] * has_upper
                    code[z + 2, b, end : end + CODE_HALO] = upper[z, a:c].astype(jnp.int32)
                    target[z, b, end : end + FIXED_HALO] = upper[z, c:d]
                place_edge(z, slice(0, HALO), lower_corner[z], has_lower)
                place_edge(z, slice(end, end + HALO), upper_corner[z], has_upper)
                return 0

            lax.fori_loop(0, planes, plane, 0, unroll=True)

        even = at_x % 2 == 0
        pl.when(even)(functools.partial(place_rows, across, pair, across_corner, pair_corner))
        pl.when(jnp.logical_not(even))(functools.partial(place_rows, pair, across, pair_corner, across_corner))

    def fill_table(source, table, starts):
        def plane(z, _):
            for x in starts:
                at, up = group(x), group(x + 1)
                sums = [
                    (Z0 * X0) * source[z, b, at]
                    + (Z0 * X1) * source[z, b, up]
                    + (Z1 * X0) * source[z + 1, b, at]
                    + (Z1 * X1) * source[z + 1, b, up]
                    for b in range(blocks)
                ]
                moved = {step: shifted(sums, step, lane) for step in range(-2, 3)}
                for o in range(4):
                    for b in range(blocks):
                        table[o, z + 1, b, at] = Y0 * moved[o - 2][b] + Y1 * moved[o - 1][b]
            return 0

        lax.fori_loop(0, planes + 1, plane, 0, unroll=True)

    def masks(value):
        return [(value & (1 << bit)) != 0 for bit in range(6)]

    def choose(options, low, high):
        return jnp.where(high, jnp.where(low, options[3], options[2]), jnp.where(low, options[1], options[0]))

    def pick(table, z, b, x, bits):
        together = len(bits)
        found = [[] for _ in bits]
        for p in range(together + 3):
            users = [j for j in range(together) if 0 <= p - j < 4]
            lines = [[] for _ in bits]
            for ox in range(4):
                at = group(x + ox - 2)
                options = [table[oy, z + p, b, at] for oy in range(4)]
                for j in users:
                    lines[j].append(choose(options, bits[j][0], bits[j][1]))
            for j in users:
                found[j].append(choose(lines[j], bits[j][2], bits[j][3]))
        return [choose(found[j], bits[j][4], bits[j][5]) for j in range(together)]

    def transport_once(starts):
        def first_planes(turn, _):
            z, b = 0, turn
            for x in starts:
                values = pick(table, z, b, x, [masks(code[z + j + 2, b, group(x)]) for j in range(planes)])
                for j, value in enumerate(values):
                    first[z + j + 1, b, group(x)] = inside(value, x, b)
            return 0

        lax.fori_loop(0, blocks, first_planes, 0)

    def transport_twice(starts):
        def second_planes(turn, _):
            z, b = 0, turn
            for x in starts:
                at = group(x)
                spots = [code[z + j + 2, b, at] for j in range(planes)]
                values = pick(second, z, b, x, [masks(spot) for spot in spots])
                for j, (spot, value) in enumerate(zip(spots, values)):
                    value = inside(value - target[z + j, b, at], x, b)
                    last[z + j, b, at] = value
                    along = spot & 3
                    for o in range(4):
                        parts[o, z + j + 2, b, at] = jnp.where(along == o, value, 0.0)
                    code[z + j + 2, b, at] = lax.shift_right_logical(spot, 2)
            return 0

        lax.fori_loop(0, blocks, second_planes, 0)

    def land(starts):
        def land_planes(turn, _):
            z = turn * 3
            for b in range(blocks):
                for x in starts:
                    sums = [[None] * 4 for _ in range(3)]
                    for p in range(3 + 3):
                        for ox in range(4):
                            at = group(x + 2 - ox)
                            spot = code[z + p, b, at]
                            values = [parts[oy, z + p, b, at] for oy in range(4)]
                            for j in range(3):
                                oz = j + 3 - p
                                if not 0 <= oz < 4:
                                    continue
                                here = spot == oz * 4 + ox
                                for oy in range(4):
                                    term = jnp.where(here, values[oy], 0.0)
                                    sums[j][oy] = term if sums[j][oy] is None else sums[j][oy] + term
                    for j in range(3):
                        for oy in range(4):
                            landed[oy, z + j, b, group(x)] = sums[j][oy]
            return 0

        lax.fori_loop(0, (planes + 1) // 3, land_planes, 0)

    def finish(out, carried, raw):
        for k in range(3):
            for spot in (0, 1, planes + 2, planes + 3):
                raw[k, spot] = jnp.zeros((blocks, rows + 2 * HALO, LANES), f32)

        def carry_plane(z, _):
            for x in (-3, 5, 10):
                found = [[landed[oy, z, b, group(x)] for b in range(blocks)] for oy in range(4)]
                total = None
                for step in range(-2, 3):
                    low, high = step + 2, step + 1
                    terms = []
                    for b in range(blocks):
                        term = Y0 * found[low][b] if low < 4 else None
                        if high >= 0:
                            more = Y1 * found[high][b]
                            term = more if term is None else term + more
                        terms.append(term)
                    terms = shifted(terms, -step, lane)
                    total = terms if total is None else [s + t for s, t in zip(total, terms)]
                for b in range(blocks):
                    carried[z, b, group(x)] = total[b]
            return 0

        lax.fori_loop(0, planes + 1, carry_plane, 0, unroll=True)

        def raw_plane(z, _):
            for x in (-2, 6, 10):
                at, below, above = group(x), group(x - 1), group(x + 1)
                slope_one = [first[z + 1, b, at] for b in range(blocks)]
                slope_zero = [image[z + 1, b, at] for b in range(blocks)]
                slope_one = [s - t for s, t in zip(shifted(slope_one, 1, lane), shifted(slope_one, -1, lane))]
                slope_zero = [s - t for s, t in zip(shifted(slope_zero, 1, lane), shifted(slope_zero, -1, lane))]
                for b in range(blocks):
                    one = inside(last[z, b, at], x, b)
                    two = (
                        (Z0 * X0) * carried[z + 1, b, at]
                        + (Z0 * X1) * carried[z + 1, b, below]
                        + (Z1 * X0) * carried[z, b, at]
                        + (Z1 * X1) * carried[z, b, below]
                    )
                    two = inside(two, x, b)
                    raw[0, z + 2, b, at] = one * (first[z + 2, b, at] - first[z, b, at]) + two * (image[z + 2, b, at] - image[z, b, at])
                    raw[1, z + 2, b, at] = one * (first[z + 1, b, above] - first[z + 1, b, below]) + two * (
                        image[z + 1, b, above] - image[z + 1, b, below]
                    )
                    raw[2, z + 2, b, at] = one * slope_one[b] + two * slope_zero[b]
            return 0

        lax.fori_loop(0, planes, raw_plane, 0, unroll=True)

        def taps(a, b, c, d, e):
            return (a + e) + 4.0 * (b + d) + 6.0 * c

        def rows_plane(z, _):
            for k in range(3):
                for b in range(blocks):
                    for x in range(0, rows, 8):
                        table[k, z, b, group(x)] = taps(*[raw[k, z, b, group(x + s)] for s in range(-2, 3)])
            return 0

        lax.fori_loop(0, planes + 4, rows_plane, 0, unroll=True)

        scale = -0.5 / 4096.0

        def out_plane(z, _):
            for k in range(3):
                halves = []
                for x in range(0, rows, 8):
                    values = [taps(*[table[k, z + s, b, group(x)] for s in range(5)]) for b in range(blocks)]
                    moved = [shifted(values, step, lane) for step in range(-2, 3)]
                    halves.append([taps(*[m[b] for m in moved]) * scale for b in range(inner)])
                for b in range(inner):
                    both = jnp.concatenate([half[b] for half in halves], axis=0)
                    out[k, z, :, b * LANES : (b + 1) * LANES] = both.astype(out.dtype)
            return 0

        lax.fori_loop(0, planes, out_plane, 0, unroll=True)

    made = Stages()
    made.clear, made.place_inner, made.place_outer, made.fill_table = clear, place_inner, place_outer, fill_table
    made.transport_once, made.transport_twice, made.land, made.finish = transport_once, transport_twice, land, finish
    return made


def inner_cells(peers, planes, rows, inner, pair_edge, across_edge, image_in, code_in, target_in, *held):
    image, first, code, target, last, table, second, parts, landed = held
    run = stages(peers, planes, rows, inner, held)
    run.clear()
    run.place_inner(pair_edge, across_edge)
    run.fill_table(image, table, (0, 7))
    run.transport_once((2, 6))
    run.fill_table(first, second, (2, 5))
    run.transport_twice((4,))
    run.land((5,))


def outer_cells(peers, pair, across, pair_corner, across_corner, *refs):
    out, held, (carried, raw) = refs[9], refs[10:19], refs[19:]
    planes, rows, cols = out.shape[1:]
    image, first, code, target, last, table, second, parts, landed = held
    run = stages(peers, planes, rows, cols // LANES, held)
    run.place_outer(pair, across, pair_corner, across_corner)
    run.fill_table(image, table, (-8, 15))
    run.transport_once((-6, 14))
    run.fill_table(first, second, (-6, 13))
    run.transport_twice((-4, 12))
    run.land((-3, 10))
    run.finish(out, carried, raw)


def swapped(pair, across, axis, ends):
    count = lax.axis_size(axis)
    rest = [(i, i + 1) for i in range(1, count - 1, 2)] + ([(0, count - 1)] if ends else [])
    pair = lax.ppermute(pair, axis, [(i, i ^ 1) for i in range(count)])
    return pair, lax.ppermute(across, axis, rest + [(j, i) for i, j in rest])


def shards(moving, fixed, codes):
    planes, rows, cols = moving.shape
    blocks = cols // LANES + 1
    f32 = jnp.float32
    params = pltpu.CompilerParams(vmem_limit_bytes=VMEM)
    slab = jax.ShapeDtypeStruct((planes, (blocks - 1) * SLAB, LANES), f32)
    corner = jax.ShapeDtypeStruct((planes, HALO, LANES), f32)

    def space(*lead, kind=f32):
        return jax.ShapeDtypeStruct((*lead, blocks, rows + 2 * HALO, LANES), kind)

    placed = (space(planes + 2), space(planes + 4, kind=jnp.int32), space(planes))
    edge, *slabs, image, code, target = pl.pallas_call(
        pack,
        out_shape=(jax.ShapeDtypeStruct((planes, rows, LANES), f32), slab, slab, *placed),
        compiler_params=pltpu.CompilerParams(vmem_limit_bytes=PACK_VMEM),
    )(moving, fixed, codes)
    edges = swapped(edge, edge, "py", False)
    slabs = swapped(*slabs, "px", True)
    corners = pl.pallas_call(
        pack_corners,
        out_shape=(corner, corner),
        cost_estimate=pl.CostEstimate(flops=2**24, bytes_accessed=2**24, transcendentals=0),
        compiler_params=params,
    )(*edges)
    corners = swapped(*corners, "px", True)
    peers = (lax.axis_size("px"), lax.axis_size("py"))

    held = [
        space(planes + 2),
        space(planes + 2),
        space(planes + 4, kind=jnp.int32),
        space(planes),
        space(planes),
        space(4, planes + 4),
        space(4, planes + 3),
        space(4, planes + 4),
        space(4, planes + 1),
    ]
    held = pl.pallas_call(
        functools.partial(inner_cells, peers, planes, rows, blocks - 1),
        out_shape=held,
        input_output_aliases={2: 0, 3: 2, 4: 3},
        cost_estimate=pl.CostEstimate(flops=2**24, bytes_accessed=2**24, transcendentals=0),
        compiler_params=params,
    )(*edges, image, code, target)
    return pl.pallas_call(
        functools.partial(outer_cells, peers),
        out_shape=[jax.ShapeDtypeStruct((3, planes, rows, cols), jnp.bfloat16), *held],
        input_output_aliases={4 + i: 1 + i for i in range(len(held))},
        scratch_shapes=[pltpu.VMEM(a.shape, a.dtype) for a in (space(planes + 1), space(3, planes + 4))],
        compiler_params=params,
    )(*slabs, *corners, *held)[0]


def solution(mesh):
    placed = P(None, "px", "py")
    return jax.shard_map(
        shards, mesh=mesh, in_specs=(placed,) * 3, out_specs=P(None, None, "px", "py"), check_vma=False
    )
```

```python
import functools

import jax
import jax.numpy as jnp
from jax import lax
from jax.experimental import pallas as pl
from jax.experimental.pallas import tpu as pltpu
from jax.sharding import PartitionSpec as P

LANES = 128
HALO = 8
FIXED_HALO = 4
CODE_HALO = 6
SLAB = HALO + CODE_HALO + FIXED_HALO
VMEM = 32 * 1024 * 1024
PACK_VMEM = 8 * 1024 * 1024

Z1, X1, Y1 = 0.25, 0.375, 0.625
Z0, X0, Y0 = 1.0 - Z1, 1.0 - X1, 1.0 - Y1


def roll(value, shift):
    return pltpu.roll(value, shift % LANES, 1)


def shifted(blocks, step, lane, wanted=None):
    count = len(blocks)
    wanted = range(count) if wanted is None else wanted
    if step == 0:
        return {b: blocks[b] for b in wanted}
    beside = 1 if step > 0 else -1
    needed = {b % count for b in wanted} | {(b + beside) % count for b in wanted}
    rolled = {b: roll(blocks[b], -step) for b in sorted(needed)}
    keep = lane < LANES - step if step > 0 else lane >= -step
    return {b: jnp.where(keep, rolled[b], rolled[(b + beside) % count]) for b in wanted}


def merged_edge(pair, across, z, lane, even):
    left = (lane >= LANES - HALO) | ((lane >= HALO) & (lane < 2 * HALO)) | ((lane >= 3 * HALO) & (lane < 4 * HALO))
    return jnp.where(left != even, pair[z], across[z])


def pack(moving, fixed, codes, edge, pair, across, image, code_at, target_at):
    planes, rows, cols = moving.shape
    own = slice(HALO, HALO + rows)
    lane = lax.broadcasted_iota(jnp.int32, (rows, LANES), 1)

    def ring(held, z):
        return jnp.where(lane < LANES // 2, held[z, :, :LANES], held[z, :, cols - LANES :]).astype(jnp.float32)

    for z in range(planes):
        code, target = roll(ring(codes, z), 2 * HALO), roll(ring(fixed, z), 4 * HALO)
        packed = jnp.where((lane >= HALO) & (lane < 3 * HALO), code, ring(moving, z))
        edge[z] = jnp.where((lane >= 3 * HALO) & (lane < 5 * HALO), target, packed)
        for b in range(cols // LANES):
            at = slice(b * LANES, (b + 1) * LANES)
            image[z + 1, b, own] = moving[z, :, at]
            code_at[z + 2, b, own] = codes[z, :, at]
            target_at[z, b, own] = fixed[z, :, at].astype(jnp.float32)

    def slabs(first, last):
        for z in range(planes):
            for b in range(cols // LANES):
                at = slice(b * LANES, (b + 1) * LANES)
                code = codes[z, :, at].astype(jnp.float32)
                target = fixed[z, :, at].astype(jnp.float32)
                row = b * SLAB
                first[z, row : row + HALO] = moving[z, :HALO, at]
                first[z, row + HALO : row + HALO + CODE_HALO] = code[:CODE_HALO]
                first[z, row + HALO + CODE_HALO : row + SLAB] = target[:FIXED_HALO]
                last[z, row : row + HALO] = moving[z, rows - HALO :, at]
                last[z, row + HALO : row + HALO + CODE_HALO] = code[rows - CODE_HALO :]
                last[z, row + HALO + CODE_HALO : row + SLAB] = target[rows - FIXED_HALO :]

    even = lax.axis_index("px") % 2 == 0
    pl.when(even)(functools.partial(slabs, across, pair))
    pl.when(jnp.logical_not(even))(functools.partial(slabs, pair, across))


def pack_corners(pair_edge, across_edge, mark, pair, across):
    planes, rows, _ = pair_edge.shape
    lane = lax.broadcasted_iota(jnp.int32, (rows, LANES), 1)
    even_y = lax.axis_index("py") % 2 == 0

    def corners(first, last):
        for z in range(planes):
            edge = merged_edge(pair_edge, across_edge, z, lane, even_y)
            first[z] = edge[:HALO]
            last[z] = edge[rows - HALO :]

    even = lax.axis_index("px") % 2 == 0
    pl.when(even)(functools.partial(corners, across, pair))
    pl.when(jnp.logical_not(even))(functools.partial(corners, pair, across))


class Stages:
    pass


def stages(peers, planes, rows, inner, held):
    image, first, code, target, last, table, second, parts, landed = held
    blocks = inner + 1
    f32 = jnp.float32
    lane = lax.broadcasted_iota(jnp.int32, (8, LANES), 1)
    row_at = lax.broadcasted_iota(jnp.int32, (8, LANES), 0)
    at_x, at_y = lax.axis_index("px"), lax.axis_index("py")
    least = jnp.where(at_x > 0, -HALO, 0)
    most = jnp.where(at_x < peers[0] - 1, rows + HALO, rows)
    has_left = (at_y > 0).astype(f32)
    has_right = (at_y < peers[1] - 1).astype(f32)
    ring_valid = jnp.where(lane < LANES // 2, has_right, has_left)

    def inside(value, x, b):
        if x < 0 or x + 8 > rows:
            value = jnp.where((row_at + x >= least) & (row_at + x < most), value, 0.0)
        if isinstance(b, int):
            return value * ring_valid if b == inner else value
        return value * jnp.where(b == inner, ring_valid, 1.0)

    def group(x):
        return slice(x + HALO, x + HALO + 8)

    def clear():
        zeros = jnp.zeros((blocks, 32, LANES), f32)
        for ref, spots in ((image, (0, planes + 1)), (first, (0, planes + 1))):
            for spot in spots:
                ref[spot] = zeros
        for o in range(4):
            for spot in (0, planes + 2):
                table[o, spot] = zeros
                second[o, spot] = zeros
            for spot in (0, 1, planes + 2, planes + 3):
                parts[o, spot] = zeros

    own = slice(HALO, HALO + rows)
    wide_lane = lax.broadcasted_iota(jnp.int32, (rows, LANES), 1)

    def place_edge(z, at, edge, factor=1.0):
        image[z + 1, inner, at] = edge * factor
        code[z + 2, inner, at] = roll(edge, -2 * HALO).astype(jnp.int32)
        target[z, inner, at] = roll(edge, -4 * HALO)

    def place_inner(pair_edge, across_edge):
        for z in range(planes):
            place_edge(z, own, merged_edge(pair_edge, across_edge, z, wide_lane, at_y % 2 == 0))

    def place_outer(pair, across, pair_corner, across_corner):
        end = HALO + rows
        has_lower = (at_x > 0).astype(f32)
        has_upper = (at_x < peers[0] - 1).astype(f32)

        def place_rows(lower, upper, lower_corner, upper_corner):
            def plane(z, _):
                for b in range(inner):
                    row = b * SLAB
                    a = row + HALO
                    c = a + CODE_HALO
                    d = c + FIXED_HALO
                    image[z + 1, b, 0:HALO] = lower[z, row:a] * has_lower
                    code[z + 2, b, HALO - CODE_HALO : HALO] = lower[z, a:c].astype(jnp.int32)
                    target[z, b, HALO - FIXED_HALO : HALO] = lower[z, c:d]
                    image[z + 1, b, end : end + HALO] = upper[z, row:a] * has_upper
                    code[z + 2, b, end : end + CODE_HALO] = upper[z, a:c].astype(jnp.int32)
                    target[z, b, end : end + FIXED_HALO] = upper[z, c:d]
                place_edge(z, slice(0, HALO), lower_corner[z], has_lower)
                place_edge(z, slice(end, end + HALO), upper_corner[z], has_upper)
                return 0

            lax.fori_loop(0, planes, plane, 0, unroll=True)

        even = at_x % 2 == 0
        pl.when(even)(functools.partial(place_rows, across, pair, across_corner, pair_corner))
        pl.when(jnp.logical_not(even))(functools.partial(place_rows, pair, across, pair_corner, across_corner))

    def fill_table(source, table, starts, wanted=None):
        wanted = tuple(range(blocks)) if wanted is None else wanted
        used = {(b + s) % blocks for b in wanted for s in (-1, 0, 1)}
        def plane(z, _):
            for x in starts:
                at, up = group(x), group(x + 1)
                sums = [
                    (Z0 * X0) * source[z, b, at]
                    + (Z0 * X1) * source[z, b, up]
                    + (Z1 * X0) * source[z + 1, b, at]
                    + (Z1 * X1) * source[z + 1, b, up]
                    if b in used
                    else None
                    for b in range(blocks)
                ]
                moved = {step: shifted(sums, step, lane, wanted) for step in range(-2, 3)}
                for o in range(4):
                    for b in wanted:
                        table[o, z + 1, b, at] = Y0 * moved[o - 2][b] + Y1 * moved[o - 1][b]
            return 0

        lax.fori_loop(0, planes + 1, plane, 0, unroll=True)

    def masks(value):
        return [(value & (1 << bit)) != 0 for bit in range(6)]

    def choose(options, low, high):
        return jnp.where(high, jnp.where(low, options[3], options[2]), jnp.where(low, options[1], options[0]))

    def pick(table, z, b, x, bits):
        together = len(bits)
        found = [[] for _ in bits]
        for p in range(together + 3):
            users = [j for j in range(together) if 0 <= p - j < 4]
            lines = [[] for _ in bits]
            for ox in range(4):
                at = group(x + ox - 2)
                options = [table[oy, z + p, b, at] for oy in range(4)]
                for j in users:
                    lines[j].append(choose(options, bits[j][0], bits[j][1]))
            for j in users:
                found[j].append(choose(lines[j], bits[j][2], bits[j][3]))
        return [choose(found[j], bits[j][4], bits[j][5]) for j in range(together)]

    def transport_once(starts, low=0, high=blocks):
        def first_planes(turn, _):
            z, b = 0, lax.rem(turn, blocks)
            for x in starts:
                values = pick(table, z, b, x, [masks(code[z + j + 2, b, group(x)]) for j in range(planes)])
                for j, value in enumerate(values):
                    first[z + j + 1, b, group(x)] = inside(value, x, b)
            return 0

        lax.fori_loop(low, high, first_planes, 0)

    def transport_twice(starts):
        def second_planes(turn, _):
            z, b = 0, turn
            for x in starts:
                at = group(x)
                spots = [code[z + j + 2, b, at] for j in range(planes)]
                values = pick(second, z, b, x, [masks(spot) for spot in spots])
                for j, (spot, value) in enumerate(zip(spots, values)):
                    value = inside(value - target[z + j, b, at], x, b)
                    last[z + j, b, at] = value
                    along = spot & 3
                    for o in range(4):
                        parts[o, z + j + 2, b, at] = jnp.where(along == o, value, 0.0)
                    code[z + j + 2, b, at] = lax.shift_right_logical(spot, 2)
            return 0

        lax.fori_loop(0, blocks, second_planes, 0)

    def land(starts):
        def land_planes(turn, _):
            z = turn * 3
            for b in range(blocks):
                for x in starts:
                    sums = [[None] * 4 for _ in range(3)]
                    for p in range(3 + 3):
                        for ox in range(4):
                            at = group(x + 2 - ox)
                            spot = code[z + p, b, at]
                            values = [parts[oy, z + p, b, at] for oy in range(4)]
                            for j in range(3):
                                oz = j + 3 - p
                                if not 0 <= oz < 4:
                                    continue
                                here = spot == oz * 4 + ox
                                for oy in range(4):
                                    term = jnp.where(here, values[oy], 0.0)
                                    sums[j][oy] = term if sums[j][oy] is None else sums[j][oy] + term
                    for j in range(3):
                        for oy in range(4):
                            landed[oy, z + j, b, group(x)] = sums[j][oy]
            return 0

        lax.fori_loop(0, (planes + 1) // 3, land_planes, 0)

    def finish(out, carried, raw):
        for k in range(3):
            for spot in (0, 1, planes + 2, planes + 3):
                raw[k, spot] = jnp.zeros((blocks, rows + 2 * HALO, LANES), f32)

        def carry_plane(z, _):
            for x in (-3, 5, 10):
                found = [[landed[oy, z, b, group(x)] for b in range(blocks)] for oy in range(4)]
                total = None
                for step in range(-2, 3):
                    low, high = step + 2, step + 1
                    terms = []
                    for b in range(blocks):
                        term = Y0 * found[low][b] if low < 4 else None
                        if high >= 0:
                            more = Y1 * found[high][b]
                            term = more if term is None else term + more
                        terms.append(term)
                    moved = shifted(terms, -step, lane)
                    terms = [moved[b] for b in range(blocks)]
                    total = terms if total is None else [s + t for s, t in zip(total, terms)]
                for b in range(blocks):
                    carried[z, b, group(x)] = total[b]
            return 0

        lax.fori_loop(0, planes + 1, carry_plane, 0, unroll=True)

        def difference(values):
            ahead, behind = shifted(values, 1, lane), shifted(values, -1, lane)
            return [ahead[b] - behind[b] for b in range(blocks)]

        def raw_plane(z, _):
            for x in (-2, 6, 10):
                at, below, above = group(x), group(x - 1), group(x + 1)
                slope_one = [first[z + 1, b, at] for b in range(blocks)]
                slope_zero = [image[z + 1, b, at] for b in range(blocks)]
                slope_one = difference(slope_one)
                slope_zero = difference(slope_zero)
                for b in range(blocks):
                    one = inside(last[z, b, at], x, b)
                    two = (
                        (Z0 * X0) * carried[z + 1, b, at]
                        + (Z0 * X1) * carried[z + 1, b, below]
                        + (Z1 * X0) * carried[z, b, at]
                        + (Z1 * X1) * carried[z, b, below]
                    )
                    two = inside(two, x, b)
                    raw[0, z + 2, b, at] = one * (first[z + 2, b, at] - first[z, b, at]) + two * (image[z + 2, b, at] - image[z, b, at])
                    raw[1, z + 2, b, at] = one * (first[z + 1, b, above] - first[z + 1, b, below]) + two * (
                        image[z + 1, b, above] - image[z + 1, b, below]
                    )
                    raw[2, z + 2, b, at] = one * slope_one[b] + two * slope_zero[b]
            return 0

        lax.fori_loop(0, planes, raw_plane, 0, unroll=True)

        def taps(a, b, c, d, e):
            return (a + e) + 4.0 * (b + d) + 6.0 * c

        def rows_plane(z, _):
            for k in range(3):
                for b in range(blocks):
                    for x in range(0, rows, 8):
                        table[k, z, b, group(x)] = taps(*[raw[k, z, b, group(x + s)] for s in range(-2, 3)])
            return 0

        lax.fori_loop(0, planes + 4, rows_plane, 0, unroll=True)

        scale = -0.5 / 4096.0

        def out_plane(z, _):
            for k in range(3):
                halves = []
                for x in range(0, rows, 8):
                    values = [taps(*[table[k, z + s, b, group(x)] for s in range(5)]) for b in range(blocks)]
                    moved = [shifted(values, step, lane) for step in range(-2, 3)]
                    halves.append([taps(*[m[b] for m in moved]) * scale for b in range(inner)])
                for b in range(inner):
                    both = jnp.concatenate([half[b] for half in halves], axis=0)
                    out[k, z, :, b * LANES : (b + 1) * LANES] = both.astype(out.dtype)
            return 0

        lax.fori_loop(0, planes, out_plane, 0, unroll=True)

    made = Stages()
    made.clear, made.place_inner, made.place_outer, made.fill_table = clear, place_inner, place_outer, fill_table
    made.transport_once, made.transport_twice, made.land, made.finish = transport_once, transport_twice, land, finish
    return made


def middle_cells(peers, planes, rows, inner, image_in, code, *held):
    *held, mark = held
    image, first, table, second, parts = held
    mark[...] = jnp.zeros_like(mark)
    run = stages(peers, planes, rows, inner, (image, first, code, None, None, table, second, parts, None))
    run.clear()
    run.fill_table(image, table, (0, 7), tuple(range(1, inner - 1)))
    run.transport_once((2, 6), 1, inner - 1)


def inner_cells(peers, planes, rows, inner, pair_edge, across_edge, *refs):
    held = refs[7:]
    image, first, code, target, last, table, second, parts, landed = held
    run = stages(peers, planes, rows, inner, held)
    run.place_inner(pair_edge, across_edge)
    run.fill_table(image, table, (0, 7), (inner - 1, inner, 0))
    run.transport_once((2, 6), inner - 1, inner + 2)
    run.fill_table(first, second, (2, 5))
    run.transport_twice((4,))
    run.land((5,))


def outer_cells(peers, pair, across, pair_corner, across_corner, *refs):
    out, held, (carried, raw) = refs[9], refs[10:19], refs[19:]
    planes, rows, cols = out.shape[1:]
    image, first, code, target, last, table, second, parts, landed = held
    run = stages(peers, planes, rows, cols // LANES, held)
    run.place_outer(pair, across, pair_corner, across_corner)
    run.fill_table(image, table, (-8, 15))
    run.transport_once((-6, 14))
    run.fill_table(first, second, (-6, 13))
    run.transport_twice((-4, 12))
    run.land((-3, 10))
    run.finish(out, carried, raw)


def swapped(pair, across, axis, ends):
    count = lax.axis_size(axis)
    rest = [(i, i + 1) for i in range(1, count - 1, 2)] + ([(0, count - 1)] if ends else [])
    pair = lax.ppermute(pair, axis, [(i, i ^ 1) for i in range(count)])
    return pair, lax.ppermute(across, axis, rest + [(j, i) for i, j in rest])


def shards(moving, fixed, codes):
    planes, rows, cols = moving.shape
    blocks = cols // LANES + 1
    f32 = jnp.float32
    params = pltpu.CompilerParams(vmem_limit_bytes=VMEM)
    slab = jax.ShapeDtypeStruct((planes, (blocks - 1) * SLAB, LANES), f32)
    corner = jax.ShapeDtypeStruct((planes, HALO, LANES), f32)

    def space(*lead, kind=f32):
        return jax.ShapeDtypeStruct((*lead, blocks, rows + 2 * HALO, LANES), kind)

    placed = (space(planes + 2), space(planes + 4, kind=jnp.int32), space(planes))
    edge, *slabs, image, code, target = pl.pallas_call(
        pack,
        out_shape=(jax.ShapeDtypeStruct((planes, rows, LANES), f32), slab, slab, *placed),
        compiler_params=pltpu.CompilerParams(vmem_limit_bytes=PACK_VMEM),
    )(moving, fixed, codes)
    edges = swapped(edge, edge, "py", False)
    slabs = swapped(*slabs, "px", True)
    peers = (lax.axis_size("px"), lax.axis_size("py"))

    held = [
        space(planes + 2),
        space(planes + 2),
        space(planes + 4, kind=jnp.int32),
        space(planes),
        space(planes),
        space(4, planes + 4),
        space(4, planes + 3),
        space(4, planes + 4),
        space(4, planes + 1),
    ]
    kept = [held[i] for i in (0, 1, 5, 6, 7)]
    image, first, table, second, parts, mark = pl.pallas_call(
        functools.partial(middle_cells, peers, planes, rows, blocks - 1),
        out_shape=[*kept, jax.ShapeDtypeStruct((8, LANES), f32)],
        input_output_aliases={0: 0},
        cost_estimate=pl.CostEstimate(flops=2**22, bytes_accessed=2**22, transcendentals=0),
        compiler_params=params,
    )(image, code)
    corners = pl.pallas_call(
        pack_corners,
        out_shape=(corner, corner),
        cost_estimate=pl.CostEstimate(flops=2**24, bytes_accessed=2**24, transcendentals=0),
        compiler_params=params,
    )(*edges, mark)
    corners = swapped(*corners, "px", True)
    held = pl.pallas_call(
        functools.partial(inner_cells, peers, planes, rows, blocks - 1),
        out_shape=held,
        input_output_aliases={2: 0, 3: 1, 4: 2, 5: 3, 6: 5, 7: 6, 8: 7},
        cost_estimate=pl.CostEstimate(flops=2**24, bytes_accessed=2**24, transcendentals=0),
        compiler_params=params,
    )(*edges, image, first, code, target, table, second, parts)
    return pl.pallas_call(
        functools.partial(outer_cells, peers),
        out_shape=[jax.ShapeDtypeStruct((3, planes, rows, cols), jnp.bfloat16), *held],
        input_output_aliases={4 + i: 1 + i for i in range(len(held))},
        scratch_shapes=[pltpu.VMEM(a.shape, a.dtype) for a in (space(planes + 1), space(3, planes + 4))],
        compiler_params=params,
    )(*slabs, *corners, *held)[0]


def solution(mesh):
    placed = P(None, "px", "py")
    return jax.shard_map(
        shards, mesh=mesh, in_specs=(placed,) * 3, out_specs=P(None, None, "px", "py"), check_vma=False
    )
```

```python
import functools

import jax
import jax.numpy as jnp
from jax import lax
from jax.experimental import pallas as pl
from jax.experimental.pallas import tpu as pltpu
from jax.sharding import PartitionSpec as P

LANES = 128
HALO = 8
FIXED_HALO = 4
CODE_HALO = 6
SLAB = HALO + CODE_HALO + FIXED_HALO
VMEM = 32 * 1024 * 1024
PACK_VMEM = 8 * 1024 * 1024

Z1, X1, Y1 = 0.25, 0.375, 0.625
Z0, X0, Y0 = 1.0 - Z1, 1.0 - X1, 1.0 - Y1


def roll(value, shift):
    return pltpu.roll(value, shift % LANES, 1)


def shifted(blocks, step, lane, wanted=None):
    count = len(blocks)
    wanted = range(count) if wanted is None else wanted
    if step == 0:
        return {b: blocks[b] for b in wanted}
    beside = 1 if step > 0 else -1
    needed = {b % count for b in wanted} | {(b + beside) % count for b in wanted}
    rolled = {b: roll(blocks[b], -step) for b in sorted(needed)}
    keep = lane < LANES - step if step > 0 else lane >= -step
    return {b: jnp.where(keep, rolled[b], rolled[(b + beside) % count]) for b in wanted}


def merged_edge(pair, across, z, lane, even):
    left = (lane >= LANES - HALO) | ((lane >= HALO) & (lane < 2 * HALO)) | ((lane >= 3 * HALO) & (lane < 4 * HALO))
    return jnp.where(left != even, pair[z], across[z])


def pack(moving, fixed, codes, edge, pair, across, image, code_at, target_at):
    planes, rows, cols = moving.shape
    own = slice(HALO, HALO + rows)
    lane = lax.broadcasted_iota(jnp.int32, (rows, LANES), 1)

    def ring(held, z):
        return jnp.where(lane < LANES // 2, held[z, :, :LANES], held[z, :, cols - LANES :]).astype(jnp.float32)

    for z in range(planes):
        code, target = roll(ring(codes, z), 2 * HALO), roll(ring(fixed, z), 4 * HALO)
        packed = jnp.where((lane >= HALO) & (lane < 3 * HALO), code, ring(moving, z))
        edge[z] = jnp.where((lane >= 3 * HALO) & (lane < 5 * HALO), target, packed)
        for b in range(cols // LANES):
            at = slice(b * LANES, (b + 1) * LANES)
            image[z + 1, b, own] = moving[z, :, at]
            code_at[z + 2, b, own] = codes[z, :, at]
            target_at[z, b, own] = fixed[z, :, at].astype(jnp.float32)

    def slabs(first, last):
        for z in range(planes):
            for b in range(cols // LANES):
                at = slice(b * LANES, (b + 1) * LANES)
                code = codes[z, :, at].astype(jnp.float32)
                target = fixed[z, :, at].astype(jnp.float32)
                row = b * SLAB
                first[z, row : row + HALO] = moving[z, :HALO, at]
                first[z, row + HALO : row + HALO + CODE_HALO] = code[:CODE_HALO]
                first[z, row + HALO + CODE_HALO : row + SLAB] = target[:FIXED_HALO]
                last[z, row : row + HALO] = moving[z, rows - HALO :, at]
                last[z, row + HALO : row + HALO + CODE_HALO] = code[rows - CODE_HALO :]
                last[z, row + HALO + CODE_HALO : row + SLAB] = target[rows - FIXED_HALO :]

    even = lax.axis_index("px") % 2 == 0
    pl.when(even)(functools.partial(slabs, across, pair))
    pl.when(jnp.logical_not(even))(functools.partial(slabs, pair, across))


def pack_corners(pair_edge, across_edge, mark, pair, across):
    planes, rows, _ = pair_edge.shape
    lane = lax.broadcasted_iota(jnp.int32, (rows, LANES), 1)
    even_y = lax.axis_index("py") % 2 == 0

    def corners(first, last):
        for z in range(planes):
            edge = merged_edge(pair_edge, across_edge, z, lane, even_y)
            first[z] = edge[:HALO]
            last[z] = edge[rows - HALO :]

    even = lax.axis_index("px") % 2 == 0
    pl.when(even)(functools.partial(corners, across, pair))
    pl.when(jnp.logical_not(even))(functools.partial(corners, pair, across))


class Stages:
    pass


def stages(peers, planes, rows, inner, held):
    image, first, code, target, last, table, second, parts, landed = held
    blocks = inner + 1
    f32 = jnp.float32
    lane = lax.broadcasted_iota(jnp.int32, (8, LANES), 1)
    row_at = lax.broadcasted_iota(jnp.int32, (8, LANES), 0)
    at_x, at_y = lax.axis_index("px"), lax.axis_index("py")
    least = jnp.where(at_x > 0, -HALO, 0)
    most = jnp.where(at_x < peers[0] - 1, rows + HALO, rows)
    has_left = (at_y > 0).astype(f32)
    has_right = (at_y < peers[1] - 1).astype(f32)
    ring_valid = jnp.where(lane < LANES // 2, has_right, has_left)

    def inside(value, x, b):
        if x < 0 or x + 8 > rows:
            value = jnp.where((row_at + x >= least) & (row_at + x < most), value, 0.0)
        if isinstance(b, int):
            return value * ring_valid if b == inner else value
        return value * jnp.where(b == inner, ring_valid, 1.0)

    def group(x):
        return slice(x + HALO, x + HALO + 8)

    def clear():
        zeros = jnp.zeros((blocks, 32, LANES), f32)
        for ref, spots in ((image, (0, planes + 1)), (first, (0, planes + 1))):
            for spot in spots:
                ref[spot] = zeros
        for o in range(4):
            for spot in (0, planes + 2):
                table[o, spot] = zeros
                second[o, spot] = zeros
            for spot in (0, 1, planes + 2, planes + 3):
                parts[o, spot] = zeros

    own = slice(HALO, HALO + rows)
    wide_lane = lax.broadcasted_iota(jnp.int32, (rows, LANES), 1)

    def place_edge(z, at, edge, factor=1.0):
        image[z + 1, inner, at] = edge * factor
        code[z + 2, inner, at] = roll(edge, -2 * HALO).astype(jnp.int32)
        target[z, inner, at] = roll(edge, -4 * HALO)

    def place_inner(pair_edge, across_edge):
        for z in range(planes):
            place_edge(z, own, merged_edge(pair_edge, across_edge, z, wide_lane, at_y % 2 == 0))

    def place_outer(pair, across, pair_corner, across_corner):
        end = HALO + rows
        has_lower = (at_x > 0).astype(f32)
        has_upper = (at_x < peers[0] - 1).astype(f32)

        def place_rows(lower, upper, lower_corner, upper_corner):
            def plane(z, _):
                for b in range(inner):
                    row = b * SLAB
                    a = row + HALO
                    c = a + CODE_HALO
                    d = c + FIXED_HALO
                    image[z + 1, b, 0:HALO] = lower[z, row:a] * has_lower
                    code[z + 2, b, HALO - CODE_HALO : HALO] = lower[z, a:c].astype(jnp.int32)
                    target[z, b, HALO - FIXED_HALO : HALO] = lower[z, c:d]
                    image[z + 1, b, end : end + HALO] = upper[z, row:a] * has_upper
                    code[z + 2, b, end : end + CODE_HALO] = upper[z, a:c].astype(jnp.int32)
                    target[z, b, end : end + FIXED_HALO] = upper[z, c:d]
                place_edge(z, slice(0, HALO), lower_corner[z], has_lower)
                place_edge(z, slice(end, end + HALO), upper_corner[z], has_upper)
                return 0

            lax.fori_loop(0, planes, plane, 0, unroll=True)

        even = at_x % 2 == 0
        pl.when(even)(functools.partial(place_rows, across, pair, across_corner, pair_corner))
        pl.when(jnp.logical_not(even))(functools.partial(place_rows, pair, across, pair_corner, across_corner))

    def fill_table(source, table, starts, wanted=None):
        wanted = tuple(range(blocks)) if wanted is None else wanted
        used = {(b + s) % blocks for b in wanted for s in (-1, 0, 1)}
        def plane(z, _):
            for x in starts:
                at, up = group(x), group(x + 1)
                sums = [
                    (Z0 * X0) * source[z, b, at]
                    + (Z0 * X1) * source[z, b, up]
                    + (Z1 * X0) * source[z + 1, b, at]
                    + (Z1 * X1) * source[z + 1, b, up]
                    if b in used
                    else None
                    for b in range(blocks)
                ]
                moved = {step: shifted(sums, step, lane, wanted) for step in range(-2, 3)}
                for o in range(4):
                    for b in wanted:
                        table[o, z + 1, b, at] = Y0 * moved[o - 2][b] + Y1 * moved[o - 1][b]
            return 0

        lax.fori_loop(0, planes + 1, plane, 0, unroll=True)

    def masks(value):
        return [(value & (1 << bit)) != 0 for bit in range(6)]

    def choose(options, low, high):
        return jnp.where(high, jnp.where(low, options[3], options[2]), jnp.where(low, options[1], options[0]))

    def pick(table, z, b, x, bits):
        together = len(bits)
        found = [[] for _ in bits]
        for p in range(together + 3):
            users = [j for j in range(together) if 0 <= p - j < 4]
            lines = [[] for _ in bits]
            for ox in range(4):
                at = group(x + ox - 2)
                options = [table[oy, z + p, b, at] for oy in range(4)]
                for j in users:
                    lines[j].append(choose(options, bits[j][0], bits[j][1]))
            for j in users:
                found[j].append(choose(lines[j], bits[j][2], bits[j][3]))
        return [choose(found[j], bits[j][4], bits[j][5]) for j in range(together)]

    def transport_once(starts, low=0, high=blocks):
        def first_planes(turn, _):
            z, b = 0, lax.rem(turn, blocks)
            for x in starts:
                values = pick(table, z, b, x, [masks(code[z + j + 2, b, group(x)]) for j in range(planes)])
                for j, value in enumerate(values):
                    first[z + j + 1, b, group(x)] = inside(value, x, b)
            return 0

        lax.fori_loop(low, high, first_planes, 0)

    def transport_twice(starts):
        def second_planes(turn, _):
            z, b = 0, turn
            for x in starts:
                at = group(x)
                spots = [code[z + j + 2, b, at] for j in range(planes)]
                values = pick(second, z, b, x, [masks(spot) for spot in spots])
                for j, (spot, value) in enumerate(zip(spots, values)):
                    value = inside(value - target[z + j, b, at], x, b)
                    last[z + j, b, at] = value
                    along = spot & 3
                    for o in range(4):
                        parts[o, z + j + 2, b, at] = jnp.where(along == o, value, 0.0)
                    code[z + j + 2, b, at] = lax.shift_right_logical(spot, 2)
            return 0

        lax.fori_loop(0, blocks, second_planes, 0)

    def land(starts):
        def land_planes(turn, _):
            z = turn * 3
            for b in range(blocks):
                for x in starts:
                    sums = [[None] * 4 for _ in range(3)]
                    for p in range(3 + 3):
                        for ox in range(4):
                            at = group(x + 2 - ox)
                            spot = code[z + p, b, at]
                            values = [parts[oy, z + p, b, at] for oy in range(4)]
                            for j in range(3):
                                oz = j + 3 - p
                                if not 0 <= oz < 4:
                                    continue
                                here = spot == oz * 4 + ox
                                for oy in range(4):
                                    term = jnp.where(here, values[oy], 0.0)
                                    sums[j][oy] = term if sums[j][oy] is None else sums[j][oy] + term
                    for j in range(3):
                        for oy in range(4):
                            landed[oy, z + j, b, group(x)] = sums[j][oy]
            return 0

        lax.fori_loop(0, (planes + 1) // 3, land_planes, 0)

    def finish(out, carried, raw):
        for k in range(3):
            for spot in (0, 1, planes + 2, planes + 3):
                table[k, spot, :, own] = jnp.zeros((blocks, rows, LANES), f32)

        def carry_plane(z, _):
            for x in (-3, 5, 10):
                found = [[landed[oy, z, b, group(x)] for b in range(blocks)] for oy in range(4)]
                total = None
                for step in range(-2, 3):
                    low, high = step + 2, step + 1
                    terms = []
                    for b in range(blocks):
                        term = Y0 * found[low][b] if low < 4 else None
                        if high >= 0:
                            more = Y1 * found[high][b]
                            term = more if term is None else term + more
                        terms.append(term)
                    moved = shifted(terms, -step, lane)
                    terms = [moved[b] for b in range(blocks)]
                    total = terms if total is None else [s + t for s, t in zip(total, terms)]
                for b in range(blocks):
                    carried[z, b, group(x)] = total[b]
            return 0

        lax.fori_loop(0, planes + 1, carry_plane, 0, unroll=True)

        def difference(values):
            ahead, behind = shifted(values, 1, lane), shifted(values, -1, lane)
            return [ahead[b] - behind[b] for b in range(blocks)]

        def raw_plane(z, _):
            for x in (-2, 6, 10):
                at, below, above = group(x), group(x - 1), group(x + 1)
                slope_one = [first[z + 1, b, at] for b in range(blocks)]
                slope_zero = [image[z + 1, b, at] for b in range(blocks)]
                slope_one = difference(slope_one)
                slope_zero = difference(slope_zero)
                for b in range(blocks):
                    one = inside(last[z, b, at], x, b)
                    two = (
                        (Z0 * X0) * carried[z + 1, b, at]
                        + (Z0 * X1) * carried[z + 1, b, below]
                        + (Z1 * X0) * carried[z, b, at]
                        + (Z1 * X1) * carried[z, b, below]
                    )
                    two = inside(two, x, b)
                    raw[0, z + 2, b, at] = one * (first[z + 2, b, at] - first[z, b, at]) + two * (image[z + 2, b, at] - image[z, b, at])
                    raw[1, z + 2, b, at] = one * (first[z + 1, b, above] - first[z + 1, b, below]) + two * (
                        image[z + 1, b, above] - image[z + 1, b, below]
                    )
                    raw[2, z + 2, b, at] = one * slope_one[b] + two * slope_zero[b]
            return 0

        lax.fori_loop(0, planes, raw_plane, 0, unroll=True)

        def taps(a, b, c, d, e):
            return (a + e) + 4.0 * (b + d) + 6.0 * c

        def rows_plane(z, _):
            for k in range(3):
                for b in range(blocks):
                    for x in range(0, rows, 8):
                        table[k, z, b, group(x)] = taps(*[raw[k, z, b, group(x + s)] for s in range(-2, 3)])
            return 0

        lax.fori_loop(2, planes + 2, rows_plane, 0, unroll=True)

        scale = -0.5 / 4096.0

        def out_plane(z, _):
            for k in range(3):
                halves = []
                for x in range(0, rows, 8):
                    values = [taps(*[table[k, z + s, b, group(x)] for s in range(5)]) for b in range(blocks)]
                    moved = [shifted(values, step, lane) for step in range(-2, 3)]
                    halves.append([taps(*[m[b] for m in moved]) * scale for b in range(inner)])
                for b in range(inner):
                    both = jnp.concatenate([half[b] for half in halves], axis=0)
                    out[k, z, :, b * LANES : (b + 1) * LANES] = both.astype(out.dtype)
            return 0

        lax.fori_loop(0, planes, out_plane, 0, unroll=True)

    made = Stages()
    made.clear, made.place_inner, made.place_outer, made.fill_table = clear, place_inner, place_outer, fill_table
    made.transport_once, made.transport_twice, made.land, made.finish = transport_once, transport_twice, land, finish
    return made


def middle_cells(peers, planes, rows, inner, image_in, code, *held):
    *held, mark = held
    image, first, table, second, parts = held
    mark[...] = jnp.zeros_like(mark)
    run = stages(peers, planes, rows, inner, (image, first, code, None, None, table, second, parts, None))
    run.clear()
    run.fill_table(image, table, (0, 7), tuple(range(1, inner - 1)))
    run.transport_once((2, 6), 1, inner - 1)


def inner_cells(peers, planes, rows, inner, pair_edge, across_edge, *refs):
    held = refs[7:]
    image, first, code, target, last, table, second, parts, landed = held
    run = stages(peers, planes, rows, inner, held)
    run.place_inner(pair_edge, across_edge)
    run.fill_table(image, table, (0, 7), (inner - 1, inner, 0))
    run.transport_once((2, 6), inner - 1, inner + 2)
    run.fill_table(first, second, (2, 5))
    run.transport_twice((4,))
    run.land((5,))


def outer_cells(peers, pair, across, pair_corner, across_corner, *refs):
    out, held, (carried, raw) = refs[9], refs[10:19], refs[19:]
    planes, rows, cols = out.shape[1:]
    image, first, code, target, last, table, second, parts, landed = held
    run = stages(peers, planes, rows, cols // LANES, held)
    run.place_outer(pair, across, pair_corner, across_corner)
    run.fill_table(image, table, (-8, 15))
    run.transport_once((-6, 14))
    run.fill_table(first, second, (-6, 13))
    run.transport_twice((-4, 12))
    run.land((-3, 10))
    run.finish(out, carried, raw)


def swapped(pair, across, axis, ends):
    count = lax.axis_size(axis)
    rest = [(i, i + 1) for i in range(1, count - 1, 2)] + ([(0, count - 1)] if ends else [])
    pair = lax.ppermute(pair, axis, [(i, i ^ 1) for i in range(count)])
    return pair, lax.ppermute(across, axis, rest + [(j, i) for i, j in rest])


def shards(moving, fixed, codes):
    planes, rows, cols = moving.shape
    blocks = cols // LANES + 1
    f32 = jnp.float32
    params = pltpu.CompilerParams(vmem_limit_bytes=VMEM)
    slab = jax.ShapeDtypeStruct((planes, (blocks - 1) * SLAB, LANES), f32)
    corner = jax.ShapeDtypeStruct((planes, HALO, LANES), f32)

    def space(*lead, kind=f32):
        return jax.ShapeDtypeStruct((*lead, blocks, rows + 2 * HALO, LANES), kind)

    placed = (space(planes + 2), space(planes + 4, kind=jnp.int32), space(planes))
    edge, *slabs, image, code, target = pl.pallas_call(
        pack,
        out_shape=(jax.ShapeDtypeStruct((planes, rows, LANES), f32), slab, slab, *placed),
        compiler_params=pltpu.CompilerParams(vmem_limit_bytes=PACK_VMEM),
    )(moving, fixed, codes)
    edges = swapped(edge, edge, "py", False)
    slabs = swapped(*slabs, "px", True)
    peers = (lax.axis_size("px"), lax.axis_size("py"))

    held = [
        space(planes + 2),
        space(planes + 2),
        space(planes + 4, kind=jnp.int32),
        space(planes),
        space(planes),
        space(4, planes + 4),
        space(4, planes + 3),
        space(4, planes + 4),
        space(4, planes + 1),
    ]
    kept = [held[i] for i in (0, 1, 5, 6, 7)]
    image, first, table, second, parts, mark = pl.pallas_call(
        functools.partial(middle_cells, peers, planes, rows, blocks - 1),
        out_shape=[*kept, jax.ShapeDtypeStruct((8, LANES), f32)],
        input_output_aliases={0: 0},
        cost_estimate=pl.CostEstimate(flops=2**22, bytes_accessed=2**22, transcendentals=0),
        compiler_params=params,
    )(image, code)
    corners = pl.pallas_call(
        pack_corners,
        out_shape=(corner, corner),
        cost_estimate=pl.CostEstimate(flops=2**24, bytes_accessed=2**24, transcendentals=0),
        compiler_params=params,
    )(*edges, mark)
    corners = swapped(*corners, "px", True)
    held = pl.pallas_call(
        functools.partial(inner_cells, peers, planes, rows, blocks - 1),
        out_shape=held,
        input_output_aliases={2: 0, 3: 1, 4: 2, 5: 3, 6: 5, 7: 6, 8: 7},
        cost_estimate=pl.CostEstimate(flops=2**24, bytes_accessed=2**24, transcendentals=0),
        compiler_params=params,
    )(*edges, image, first, code, target, table, second, parts)
    return pl.pallas_call(
        functools.partial(outer_cells, peers),
        out_shape=[jax.ShapeDtypeStruct((3, planes, rows, cols), jnp.bfloat16), *held],
        input_output_aliases={4 + i: 1 + i for i in range(len(held))},
        scratch_shapes=[pltpu.VMEM(a.shape, a.dtype) for a in (space(planes + 1), space(3, planes + 4))],
        compiler_params=params,
    )(*slabs, *corners, *held)[0]


def solution(mesh):
    placed = P(None, "px", "py")
    return jax.shard_map(
        shards, mesh=mesh, in_specs=(placed,) * 3, out_specs=P(None, None, "px", "py"), check_vma=False
    )
```
